128 devices in a mesh: seq: 16 (over y, z), req: 8 (over x, core).
Axes of the slice: x: 4, y: 4, z: 4, core: 2. Of those that a mesh axis runs over, the one named last changes fastest.
Arguments:
- span_queries: bfloat16 [1024, 8192], P('seq', 'req'), may hold values from -540 to 540
- span_key_value: bfloat16 [2, 1024, 1024], P(None, 'seq', 'req'), may hold values from -6 to 6
- prompt_key_value: bfloat16 [2, 16384, 1024], P(None, 'seq', 'req'), may hold values from -6 to 6
- span_start: int32 [1], replicated, may hold values from 15361 to 16384
- block_pool_key_value: bfloat16 [2048, 2, 64, 1024], P(('seq', 'req')), may hold values from -6 to 6
- block_dest: int32 [2048, 1], P(('seq', 'req')), may hold values from 0 to 15; in each aligned block of 16 rows (0 to 15, 16 to 31, ...) at most 4 rows name the same one
- block_request: int32 [2048], P(('seq', 'req')), may hold values from 0 to 1
- block_fill: int32 [2048], P(('seq', 'req')), may hold values from 1 to 64
- decode_query: bfloat16 [4, 256, 8192], P(None, ('seq', 'req')), may hold values from -540 to 540
- decoded_key_value: bfloat16 [4, 2, 256, 1024], P(None, None, ('seq', 'req')), may hold values from -6 to 6
Outputs:
- attended: bfloat16 [1024, 8192], P('seq', 'req')
- dec_out: bfloat16 [4, 256, 8192], P(None, ('seq', 'req'))
The draws below stay inside these ranges and needn't reach their ends.
Inputs may be any that keep to these rules, and one draw needn't show every extreme that they name: `block_dest`: among the rows of one device no seq index is named more than 4 times, and one is named exactly 4 times.
All inputs are finite; a program needn't handle non-finite values.
Results may differ from the reference program's by a relative error of at most 0.0044.
Values may be sent and summed in bfloat16 or wider, within the bound.
A program may use at most 320 MiB of HBM per device.

```python
import math
import jax
import jax.numpy as jnp
import numpy as np
from jax import lax

QUERY_HEADS = 64
KEY_HEADS = 8
HEAD_WIDTH = 128
SPAN_TOKENS = 1024
SHARD_LENGTH = 1024
DECODE_STEPS = 4
RQ_DEV = 2
BLOCK_SLOTS = 64
POOL_BLOCKS = 16
CAP = 4
PROMPT_LENGTH = 16384
REQUEST_TOTAL = 256
N_SEQ = 16
N_REQ = 8


def scaled_normal(key, shape):
    first = jax.random.fold_in(key, 0)
    value_rows = 3.0 * jnp.clip(jax.random.normal(first, shape, jnp.float32), -6.0, 6.0)
    return value_rows


def draw_span_queries(key, part):
    key = jax.random.fold_in(key, 11)
    value_rows = scaled_normal(key, (SPAN_TOKENS, QUERY_HEADS * HEAD_WIDTH))
    return value_rows.astype(jnp.bfloat16)


def draw_decode_query(key, part):
    key = jax.random.fold_in(key, 23)
    value_rows = scaled_normal(key, (DECODE_STEPS, REQUEST_TOTAL, QUERY_HEADS * HEAD_WIDTH))
    return value_rows.astype(jnp.bfloat16)


def touch_ends(array, stream_key, least, top_value):
    dims = array.shape
    index_at = [jax.random.randint(jax.random.fold_in(stream_key, axis), (), 0, dims[axis]) for axis in range(len(dims))]
    array = array.at[tuple(index_at)].set(least)
    longest = dims.index(max(dims))
    index_at[longest] = (index_at[longest] + 1) % dims[longest]
    return array.at[tuple(index_at)].set(top_value)


def shard_levels(key, extent, shards, smallest, largest):
    gain = 1.0
    for dim, blocks in shards:
        steps = jax.random.uniform(jax.random.fold_in(jax.random.fold_in(key, 6), dim), (blocks,), jnp.float32, smallest / len(shards), largest / len(shards))
        gain = gain * jnp.repeat(jnp.exp(steps), extent[dim] // blocks).reshape((-1,) + (1,) * (len(extent) - 1 - dim))
    return gain


def deal_out(stream_key, own, number, rows, number_of, top, reach, slope):
    sequence = jax.random.permutation(stream_key, number_of)
    heavy_load, ordinary = portions_of(number_of, rows * top, reach, slope, True), portions_of(number_of, rows * top, reach, slope, False)
    places = jnp.arange(number_of)

    def named(tallies, rotation):
        used = int((tallies > 0).sum())
        fixed = max(1, used // 4)
        moved = fixed + (places - fixed + rotation * (used - fixed)) % max(1, number_of - fixed)
        return jnp.zeros((number_of,), jnp.int32).at[sequence[jnp.where(places < fixed, places, moved)]].set(jnp.asarray(tallies, jnp.int32))

    tallies = jnp.where(number % 4 == 0, named(heavy_load, number // 4), named(ordinary, number - number // 4 - 1))
    mixed = jax.random.permutation(jax.random.fold_in(own, 3), number_of)
    donor, sink = mixed[0:number_of // 2 * 2:2], mixed[1:number_of // 2 * 2:2]
    slack = jnp.minimum(tallies[donor] - 1, reach - tallies[sink]) // 2
    slack = jnp.where((donor == sequence[0]) | (sink == sequence[0]) | (tallies[sink] == 0), 0, jnp.maximum(slack, 0))
    moved = jax.random.randint(jax.random.fold_in(own, 4), (number_of // 2,), 0, 1 << 20) % (slack + 1)
    tallies = tallies.at[donor].add(-moved).at[sink].add(moved)
    labels = jnp.searchsorted(jnp.cumsum(tallies), jnp.arange(rows * top), side="right").astype(jnp.int32)
    listing = labels.reshape(top, rows).T
    listing = listing[jax.random.permutation(jax.random.fold_in(own, 1), rows)]
    rotation = jax.random.randint(jax.random.fold_in(own, 2), (rows, 1), 0, top)
    return jnp.take_along_axis(listing, (jnp.arange(top)[None, :] + rotation) % top, axis=1)


def portions_of(count, total, bound, lean, full):
    weights = [(1 << 20) // math.isqrt(rank ** lean) + 1 for rank in range(1, count + 1)]
    largest = bound if full else min(bound, max(-(-total // count), total * weights[0] // sum(weights)))
    least = 1 if total - largest >= count - 1 else 0
    holding, rest = [largest] + [least] * (count - 1), total - largest - least * (count - 1)
    while rest > 0:
        free = [i for i in range(1, count) if holding[i] < largest] or [i for i in range(1, count) if holding[i] < bound]
        whole, left = sum([weights[i] for i in free]), rest
        for i in free:
            addition = min(bound - holding[i], max(1, left * weights[i] // whole), rest)
            holding[i] = holding[i] + addition
            rest = rest - addition
    return np.array(holding)


def gaussian(stream_key, extent, spread, reach, shards=(), kind=jnp.bfloat16):
    gain = shard_levels(stream_key, extent, shards, -0.22, 0.18) if shards else 1.0
    drawn = jax.random.normal(stream_key, extent, jnp.float32) * spread * gain
    return jnp.minimum(jnp.maximum(drawn, -reach), reach).astype(kind)


def setup_inputs(seed: int = 0) -> dict:
    keys = jax.random.split(jax.random.key(seed), 11)
    span_queries = draw_span_queries(jax.random.fold_in(keys[10], 71), 0)
    span_key_value = gaussian(keys[1], (2, SPAN_TOKENS, KEY_HEADS * HEAD_WIDTH), 1.0, 6.0, ((1, 16), (2, 8)))
    prompt_key_value = gaussian(keys[2], (2, PROMPT_LENGTH, KEY_HEADS * HEAD_WIDTH), 1.0, 6.0, ((1, 16), (2, 8)))
    span_start = jax.random.randint(keys[3], (1,), PROMPT_LENGTH - SHARD_LENGTH + 1, PROMPT_LENGTH + 1).astype(jnp.int32)
    block_pool_key_value = gaussian(keys[4], (N_SEQ * N_REQ * POOL_BLOCKS, 2, BLOCK_SLOTS, KEY_HEADS * HEAD_WIDTH), 1.0, 6.0, ((0, 128),))
    block_dest_keys = jax.random.split(jax.random.fold_in(keys[5], 1), (N_SEQ * N_REQ * POOL_BLOCKS) // POOL_BLOCKS)
    block_dest_turns = jax.random.permutation(jax.random.fold_in(keys[5], 3), (N_SEQ * N_REQ * POOL_BLOCKS) // POOL_BLOCKS)
    block_dest = jax.vmap(lambda own, number: deal_out(jax.random.fold_in(keys[5], 2), own, number, POOL_BLOCKS, N_SEQ, 1, CAP, 2))(block_dest_keys, block_dest_turns).reshape((N_SEQ * N_REQ * POOL_BLOCKS, 1))
    block_request = touch_ends(jax.random.randint(keys[6], (N_SEQ * N_REQ * POOL_BLOCKS,), 0, RQ_DEV), jax.random.fold_in(keys[6], 1), 0, RQ_DEV - 1).astype(jnp.int32)
    block_fill = touch_ends(jax.random.randint(keys[7], (N_SEQ * N_REQ * POOL_BLOCKS,), 1, BLOCK_SLOTS + 1), jax.random.fold_in(keys[7], 1), 1, BLOCK_SLOTS).astype(jnp.int32)
    decode_query = draw_decode_query(jax.random.fold_in(keys[10], 71), 0)
    decoded_key_value = gaussian(keys[9], (DECODE_STEPS, 2, REQUEST_TOTAL, KEY_HEADS * HEAD_WIDTH), 1.0, 6.0, ((2, 128),))
    return {"span_queries": span_queries, "span_key_value": span_key_value, "prompt_key_value": prompt_key_value, "span_start": span_start, "block_pool_key_value": block_pool_key_value, "block_dest": block_dest, "block_request": block_request, "block_fill": block_fill, "decode_query": decode_query, "decoded_key_value": decoded_key_value}


MASK_NEGATIVE = -1e30


def fold_pair(first, second):
    max_one, sum_one, acc_one = first
    max_two, sum_two, acc_two = second
    joined = jnp.maximum(max_one, max_two)
    scale_one = jnp.exp(max_one - joined)
    scale_two = jnp.exp(max_two - joined)
    return (joined, sum_one * scale_one + sum_two * scale_two,
            acc_one * scale_one[..., None] + acc_two * scale_two[..., None])


def soft_partial(scores, valid):
    masked = jnp.where(valid, scores, MASK_NEGATIVE)
    block_max = jnp.max(masked, axis=-1)
    probs = jnp.where(valid, jnp.exp(masked - block_max[..., None]), 0.0)
    block_sum = jnp.sum(probs, axis=-1)
    rounded = lax.optimization_barrier(probs.astype(jnp.bfloat16))
    return block_max, block_sum, rounded.astype(jnp.float32)


def reference(span_queries, span_key_value, prompt_key_value, span_start, block_pool_key_value, block_dest, block_request, block_fill, decode_query, decoded_key_value):
    head_group = QUERY_HEADS // KEY_HEADS
    scale = HEAD_WIDTH ** -0.5
    query_vector = span_queries.astype(jnp.float32).reshape(SPAN_TOKENS, KEY_HEADS, head_group, HEAD_WIDTH)
    shard_list = jnp.transpose(prompt_key_value.reshape(2, N_SEQ, SHARD_LENGTH, KEY_HEADS, HEAD_WIDTH), (1, 0, 2, 3, 4))
    start_pos = span_start[0]

    def cache_step(carry, item):
        shard_idx, shard = item
        key_rows = shard[0].astype(jnp.float32)
        value_rows = shard[1].astype(jnp.float32)
        scores = jnp.einsum("qhgd,khd->qhgk", query_vector, key_rows) * scale
        positions = shard_idx * SHARD_LENGTH + jnp.arange(SHARD_LENGTH, dtype=jnp.int32)
        valid = (positions < start_pos)[None, None, None, :]
        block_max, block_sum, weights = soft_partial(scores, valid)
        block_acc = jnp.einsum("qhgk,khd->qhgd", weights, value_rows)
        return fold_pair(carry, (block_max, block_sum, block_acc)), None

    initial_state = (jnp.full((SPAN_TOKENS, KEY_HEADS, head_group), MASK_NEGATIVE, jnp.float32),
            jnp.zeros((SPAN_TOKENS, KEY_HEADS, head_group), jnp.float32),
            jnp.zeros((SPAN_TOKENS, KEY_HEADS, head_group, HEAD_WIDTH), jnp.float32))
    cache_part, _ = lax.scan(cache_step, initial_state, (jnp.arange(N_SEQ, dtype=jnp.int32), shard_list))
    local_keys = span_key_value[0].astype(jnp.float32).reshape(SPAN_TOKENS, KEY_HEADS, HEAD_WIDTH)
    local_values = span_key_value[1].astype(jnp.float32).reshape(SPAN_TOKENS, KEY_HEADS, HEAD_WIDTH)
    scores = jnp.einsum("qhgd,khd->qhgk", query_vector, local_keys) * scale
    rows = jnp.arange(SPAN_TOKENS, dtype=jnp.int32)
    valid = (rows[None, :] <= rows[:, None])[:, None, None, :]
    own_max, own_sum, weights = soft_partial(scores, valid)
    own_acc = jnp.einsum("qhgk,khd->qhgd", weights, local_values)
    total = fold_pair(cache_part, (own_max, own_sum, own_acc))
    attended = (total[2] / total[1][..., None]).reshape(SPAN_TOKENS, QUERY_HEADS * HEAD_WIDTH).astype(jnp.bfloat16)

    shard_count = N_SEQ * N_REQ
    decode_query_rows = decode_query.astype(jnp.float32).reshape(DECODE_STEPS, REQUEST_TOTAL, KEY_HEADS, head_group, HEAD_WIDTH)
    block_pools = block_pool_key_value.reshape(shard_count, POOL_BLOCKS, 2, BLOCK_SLOTS, KEY_HEADS, HEAD_WIDTH)
    dev_ids = jnp.arange(shard_count * POOL_BLOCKS, dtype=jnp.int32) // POOL_BLOCKS
    owners = ((block_dest[:, 0] * N_REQ + dev_ids % N_REQ) * RQ_DEV + block_request).reshape(shard_count, POOL_BLOCKS)
    fills = block_fill.reshape(shard_count, POOL_BLOCKS)

    def dec_step(carry, item):
        block_list, owner_ids, fill_counts = item
        chosen = jnp.take(decode_query_rows, owner_ids, axis=1)
        key_rows = block_list[:, 0].astype(jnp.float32)
        value_rows = block_list[:, 1].astype(jnp.float32)
        scores = jnp.einsum("tbhgd,bkhd->bthgk", chosen, key_rows) * scale
        valid = (jnp.arange(BLOCK_SLOTS, dtype=jnp.int32)[None, :] < fill_counts[:, None])[:, None, None, None, :]
        block_max, block_sum, weights = soft_partial(scores, valid)
        block_acc = jnp.einsum("bthgk,bkhd->bthgd", weights, value_rows)
        run_max, run_sum, run_acc = carry
        new_max = run_max.at[owner_ids].max(block_max)
        factor = jnp.exp(block_max - new_max[owner_ids])
        keep = jnp.exp(run_max - new_max)
        run_sum = run_sum * keep + jnp.zeros_like(run_sum).at[owner_ids].add(block_sum * factor)
        run_acc = run_acc * keep[..., None] + jnp.zeros_like(run_acc).at[owner_ids].add(block_acc * factor[..., None])
        return (new_max, run_sum, run_acc), None

    decode_initial = (jnp.full((REQUEST_TOTAL, DECODE_STEPS, KEY_HEADS, head_group), MASK_NEGATIVE, jnp.float32),
                jnp.zeros((REQUEST_TOTAL, DECODE_STEPS, KEY_HEADS, head_group), jnp.float32),
                jnp.zeros((REQUEST_TOTAL, DECODE_STEPS, KEY_HEADS, head_group, HEAD_WIDTH), jnp.float32))
    dec_part, _ = lax.scan(dec_step, decode_initial, (block_pools, owners, fills))
    fresh_keys = decoded_key_value[:, 0].astype(jnp.float32).reshape(DECODE_STEPS, REQUEST_TOTAL, KEY_HEADS, HEAD_WIDTH)
    fresh_values = decoded_key_value[:, 1].astype(jnp.float32).reshape(DECODE_STEPS, REQUEST_TOTAL, KEY_HEADS, HEAD_WIDTH)
    scores = jnp.einsum("trhgd,urhd->rthgu", decode_query_rows, fresh_keys) * scale
    order = jnp.arange(DECODE_STEPS, dtype=jnp.int32)
    valid = (order[None, :] <= order[:, None])[None, :, None, None, :]
    new_max, new_sum, weights = soft_partial(scores, valid)
    new_acc = jnp.einsum("rthgu,urhd->rthgd", weights, fresh_values)
    total = fold_pair(dec_part, (new_max, new_sum, new_acc))
    result = total[2] / total[1][..., None]
    dec_out = jnp.transpose(result, (1, 0, 2, 3, 4)).reshape(DECODE_STEPS, REQUEST_TOTAL, QUERY_HEADS * HEAD_WIDTH).astype(jnp.bfloat16)
    return attended, dec_out
```

```python
import functools

import jax
import jax.numpy as jnp
from jax import lax
from jax.experimental import pallas as pl
from jax.experimental.pallas import tpu as pltpu
from jax.sharding import PartitionSpec as P

QUERY_HEADS = 64
KEY_HEADS = 8
HEAD_WIDTH = 128
HEAD_GROUP = QUERY_HEADS // KEY_HEADS
CAP = 4
SIDE = 4
HOMES = SIDE * SIDE

MASK_NEGATIVE = -1e30
EXP2_SCALE = HEAD_WIDTH ** (-0.5) * 1.4426950408889634
FAR_LAST = (1, 3, 2)
CHUNK = 256


def slots_kernel(dest_ref, request_ref, fill_ref, out_ref, count_ref):
    slots = HOMES * CAP

    def clear(i, _):
        out_ref[i] = 0
        out_ref[slots + i] = 0
        out_ref[2 * slots + i] = 0
        return 0

    lax.fori_loop(0, slots, clear, 0)
    for home in range(HOMES):
        count_ref[home] = 0

    def place(block, _):
        home = dest_ref[block]
        count = count_ref[home]
        slot = home * CAP + count
        out_ref[slot] = block
        out_ref[slots + slot] = request_ref[block]
        out_ref[2 * slots + slot] = fill_ref[block]
        count_ref[home] = count + 1
        return 0

    lax.fori_loop(0, dest_ref.shape[0], place, 0)


def block_slots(dest, request, fill):
    smem = pl.BlockSpec(memory_space=pltpu.SMEM)
    return pl.pallas_call(
        slots_kernel,
        out_shape=jax.ShapeDtypeStruct((3 * HOMES * CAP,), jnp.int32),
        in_specs=[smem] * 3,
        out_specs=smem,
        scratch_shapes=[pltpu.SMEM((HOMES,), jnp.int32)],
        name="block_slots",
    )(dest, request, fill)


def dot_nt(a, b):
    return lax.dot_general(a, b, (((1,), (1,)), ((), ())), preferred_element_type=jnp.float32)


def dot_nn(a, b):
    return lax.dot_general(a, b, (((1,), (0,)), ((), ())), preferred_element_type=jnp.float32)


def packed_stats(top, total):
    lane = lax.broadcasted_iota(jnp.int32, top.shape, 1)
    return jnp.where(lane < 4, top, total)


def merge(stats, parts):
    rows = stats[0].shape[1]
    tops = [jnp.broadcast_to(s[0:1], (8, rows)) for s in stats]
    sums = [jnp.broadcast_to(s[4:5], (8, rows)) for s in stats]
    top = functools.reduce(jnp.maximum, tops)
    weights = [jnp.exp2((t - top) * EXP2_SCALE) * s for t, s in zip(tops, sums)]
    total = functools.reduce(jnp.add, weights)
    inverse = 1.0 / jnp.where(total > 0.0, total, 1.0)
    out = None
    for weight, part in zip(weights, parts):
        share = jnp.broadcast_to((weight * inverse)[0:1], (128, rows))
        term = jnp.transpose(share) * part().astype(jnp.float32)
        out = term if out is None else out + term
    sub = lax.broadcasted_iota(jnp.int32, (8, rows), 0)
    return out, jnp.where(sub < 4, top, total)


def fused_kernel(
    sq_ref, skv_ref, pkv_ref, start_ref, pool_ref, slots_ref, dq_ref, dkv_ref,
    att_ref, dec_ref,
    qb, kv, kvs, vv, dqb, pool, acc, mx, col,
    pout, pst, pin, pinst,
    aout, aost, ain, ainst,
    bout, bost, bin_, binst,
    own_out,
    pool_sem, q_s, q_r, kv_s, kv_r, ks_s, ks_r, d_s, d_r, p_s, p_r, a_s, a_r, b_s, b_r,
):
    me = lax.axis_index("seq")
    y, z = me // SIDE, me % SIDE
    rows = sq_ref.shape[0]
    block = KEY_HEADS * rows
    keys = pkv_ref.shape[1]
    mesh_id = pl.DeviceIdType.MESH

    def at(dy, dz):
        return {"seq": (y + dy) % SIDE * SIDE + (z + dz) % SIDE}

    def remote(src, dst, send, recv, dy, dz):
        return pltpu.make_async_remote_copy(
            src_ref=src, dst_ref=dst, send_sem=send, recv_sem=recv,
            device_id=at(dy, dz), device_id_type=mesh_id,
        )

    pool_copy = pltpu.make_async_copy(pool_ref, pool, pool_sem)
    pool_copy.start()

    barrier = pltpu.get_barrier_semaphore()
    for o in (1, 2, 3):
        pl.semaphore_signal(barrier, inc=1, device_id=at(o, 0), device_id_type=mesh_id)
        pl.semaphore_signal(barrier, inc=1, device_id=at(0, o), device_id_type=mesh_id)

    for h in range(KEY_HEADS):
        qb[0, pl.ds(h * rows, rows), :] = sq_ref[:, pl.ds(h * HEAD_WIDTH, HEAD_WIDTH)]
    dqb[0, 0] = dq_ref[...]
    kvs[:, pl.ds(0, rows), :] = skv_ref[...]
    start = start_ref[0]
    position = me * keys + lax.broadcasted_iota(jnp.int32, (keys, HEAD_WIDTH), 0)
    own_keys = pkv_ref[0].astype(jnp.float32)
    kv[0, 0] = jnp.where(position < start, own_keys, own_keys[0:1]).astype(jnp.bfloat16)
    kv[0, 1] = jnp.where(position < start, pkv_ref[1].astype(jnp.float32), 0.0).astype(jnp.bfloat16)

    pl.semaphore_wait(barrier, 6)

    q_c, kv_c, ks_c, d_c, p_c, a_c, b_c = {}, {}, {}, {}, {}, {}, {}
    for o in FAR_LAST:
        q_c[o] = remote(qb.at[0], qb.at[o], q_s.at[o], q_r.at[o], o, 0)
        q_c[o].start()
        d_c[0, o] = remote(dqb.at[0, 0], dqb.at[0, o], d_s.at[0, o], d_r.at[0, o], 0, o)
        d_c[0, o].start()
    for o in FAR_LAST:
        d_c[o, 0] = remote(dqb.at[0, 0], dqb.at[o, 0], d_s.at[o, 0], d_r.at[o, 0], o, 0)
        d_c[o, 0].start()
        kv_c[o] = remote(kv.at[0], kv.at[o], kv_s.at[o], kv_r.at[o], 0, o)
        kv_c[o].start()
        ks_c[o] = remote(
            skv_ref, kvs.at[:, pl.ds(o * rows, rows), :], ks_s.at[o], ks_r.at[o], 0, o
        )
        ks_c[o].start()

    def load_values(oz):
        shard = y * SIDE + (z - oz + SIDE) % SIDE
        position = shard * keys + lax.broadcasted_iota(jnp.int32, (keys, HEAD_WIDTH), 0)
        vv[:, 0:HEAD_WIDTH] = kv[oz, 1]
        vv[:, HEAD_WIDTH:] = jnp.where(position < start, 1.0, 0.0).astype(jnp.bfloat16)

    def prompt_block(oz, oy_first, oy_count, first):
        def step(i, _):
            oy = oy_first + i // (block // CHUNK)
            here = pl.ds(pl.multiple_of(i % (block // CHUNK) * CHUNK, CHUNK), CHUNK)
            s = dot_nt(qb[oy, here, :], kv[oz, 0])
            top = jnp.broadcast_to(jnp.max(s, axis=1, keepdims=True), (CHUNK, HEAD_WIDTH))
            if not first:
                old = mx[oy, here, :]
                top = jnp.maximum(old, top)
            wide = jnp.concatenate([top] * (keys // HEAD_WIDTH), axis=1)
            p = jnp.exp2((s - wide) * EXP2_SCALE).astype(jnp.bfloat16)
            o = dot_nn(p, vv[...])
            if not first:
                keep = jnp.exp2((old - top) * EXP2_SCALE)
                o = o + acc[oy, here, :] * jnp.concatenate([keep, keep], axis=1)
            acc[oy, here, :] = o
            mx[oy, here, :] = top
            return 0

        lax.fori_loop(0, oy_count * (block // CHUNK), step, 0)

    def span_block(oy):
        width = SIDE * rows
        ones = jnp.ones((width, HEAD_WIDTH), jnp.bfloat16)
        values = jnp.concatenate([kvs[1], ones], axis=1)
        row_base = ((y - oy + SIDE) % SIDE * SIDE + z) * rows

        def step(i, _):
            here = pl.ds(pl.multiple_of(i * CHUNK, CHUNK), CHUNK)
            s = dot_nt(qb[oy, here, :], kvs[0])
            row = row_base + lax.broadcasted_iota(jnp.int32, (CHUNK, width), 0) % rows
            key = lax.broadcasted_iota(jnp.int32, (CHUNK, width), 1)
            key = (y * SIDE + (z - key // rows + SIDE) % SIDE) * rows + key % rows
            valid = key <= row
            s = jnp.where(valid, s, MASK_NEGATIVE)
            old = mx[oy, here, :]
            top = jnp.maximum(
                old, jnp.broadcast_to(jnp.max(s, axis=1, keepdims=True), (CHUNK, HEAD_WIDTH))
            )
            wide = jnp.concatenate([top] * (width // HEAD_WIDTH), axis=1)
            p = jnp.where(valid, jnp.exp2((s - wide) * EXP2_SCALE), 0.0).astype(jnp.bfloat16)
            o = dot_nn(p, values)
            keep = jnp.exp2((old - top) * EXP2_SCALE)
            o = o + acc[oy, here, :] * jnp.concatenate([keep, keep], axis=1)
            total = o[:, HEAD_WIDTH:]
            pout[oy, here, :] = (o[:, :HEAD_WIDTH] / total).astype(jnp.bfloat16)
            col[here, :] = packed_stats(top, total)
            return 0

        lax.fori_loop(0, block // CHUNK, step, 0)
        pst[oy] = jnp.transpose(col[...])[0:8]

    pair_rows = block // KEY_HEADS
    window = CAP * pool.shape[2]

    def decode_home(oy, oz):
        home = (y - oy + SIDE) % SIDE * SIDE + (z - oz + SIDE) % SIDE
        first = home * CAP
        index = [slots_ref[first + c] for c in range(CAP)]
        row = lax.broadcasted_iota(jnp.int32, (pair_rows, window), 0)
        key = lax.broadcasted_iota(jnp.int32, (pair_rows, window), 1)
        which = key // pool.shape[2]
        request = jnp.zeros((pair_rows, window), jnp.int32)
        fill = jnp.zeros((pair_rows, window), jnp.int32)
        for c in range(CAP):
            request = jnp.where(which == c, slots_ref[HOMES * CAP + first + c], request)
            fill = jnp.where(which == c, slots_ref[2 * HOMES * CAP + first + c], fill)
        valid = (row // (pair_rows // 2) == request) & (key % pool.shape[2] < fill)
        valid_float = jnp.where(valid, 1.0, 0.0)
        ones = jnp.ones((window, HEAD_WIDTH), jnp.bfloat16)

        def step(h, _):
            lanes = pl.ds(pl.multiple_of(h * HEAD_WIDTH, HEAD_WIDTH), HEAD_WIDTH)
            here = pl.ds(pl.multiple_of(h * pair_rows, pair_rows), pair_rows)
            k = jnp.concatenate([pool[i, 0, :, lanes] for i in index], axis=0)
            v = jnp.concatenate([pool[i, 1, :, lanes] for i in index], axis=0)
            ok = valid_float > 0.5
            s = jnp.where(ok, dot_nt(dqb[oy, oz, here, :], k), MASK_NEGATIVE)
            top = jnp.max(s, axis=1, keepdims=True)
            p = jnp.where(ok, jnp.exp2((s - top) * EXP2_SCALE), 0.0).astype(jnp.bfloat16)
            o = dot_nn(p, jnp.concatenate([v, ones], axis=1))
            total = o[:, HEAD_WIDTH:]
            out = o[:, :HEAD_WIDTH] / jnp.where(total > 0.0, total, 1.0)
            aout[oz, oy, here, :] = out.astype(jnp.bfloat16)
            col[here, :] = packed_stats(jnp.broadcast_to(top, total.shape), total)
            return 0

        lax.fori_loop(0, KEY_HEADS, step, 0, unroll=2)
        aost[oz, oy] = jnp.transpose(col[...])[0:8]

    def send_decode(oy, oz):
        for i, (out, into) in enumerate(((aout, ain), (aost, ainst))):
            c = remote(out.at[oz, oy], into.at[oz, oy], a_s.at[oz, oy, i], a_r.at[oz, oy, i],
                       0, SIDE - oz)
            c.start()
            a_c[oz, oy, i] = c

    load_values(0)
    prompt_block(0, 0, 1, True)
    for o in FAR_LAST:
        d_c[0, o].wait_recv()
        for oy in FAR_LAST:
            d_c[oy, o] = remote(
                dqb.at[0, o], dqb.at[oy, o], d_s.at[oy, o], d_r.at[oy, o], oy, 0
            )
            d_c[oy, o].start()
    for oy in FAR_LAST:
        q_c[oy].wait_recv()
        prompt_block(0, oy, 1, True)

    pool_copy.wait()
    decode_home(0, 0)
    for oz in FAR_LAST:
        decode_home(0, oz)
        send_decode(0, oz)
    for oy in FAR_LAST:
        d_c[oy, 0].wait_recv()
        decode_home(oy, 0)

    for oz in FAR_LAST:
        kv_c[oz].wait_recv()
        load_values(oz)
        prompt_block(oz, 0, SIDE, False)
        if oz != FAR_LAST[-1]:
            for oy in FAR_LAST:
                d_c[oy, oz].wait_recv()
                decode_home(oy, oz)
                send_decode(oy, oz)

    for oz in FAR_LAST:
        ks_c[oz].wait_recv()
    for oy in (2, 1, 3):
        span_block(oy)
        for i, (out, into) in enumerate(((pout, pin), (pst, pinst))):
            c = remote(out.at[oy], into.at[oy], p_s.at[oy, i], p_r.at[oy, i], SIDE - oy, 0)
            c.start()
            p_c[oy, i] = c
    for oy in FAR_LAST:
        d_c[oy, FAR_LAST[-1]].wait_recv()
        decode_home(oy, FAR_LAST[-1])
        send_decode(oy, FAR_LAST[-1])
    span_block(0)

    extra = dkv_ref.shape[2]
    row = lax.broadcasted_iota(jnp.int32, (pair_rows, extra), 0)
    key = lax.broadcasted_iota(jnp.int32, (pair_rows, extra), 1)
    step_of_row = row % (pair_rows // 2) // HEAD_GROUP
    fresh = (row // (pair_rows // 2) == key // (extra // 2)) & (key % (extra // 2) <= step_of_row)
    ones = jnp.ones((extra, HEAD_WIDTH), jnp.bfloat16)
    for h in range(KEY_HEADS):
        here = pl.ds(h * pair_rows, pair_rows)
        s = jnp.where(fresh, dot_nt(dqb[0, 0, here, :], dkv_ref[0, h]), MASK_NEGATIVE)
        top = jnp.max(s, axis=1, keepdims=True)
        p = jnp.where(fresh, jnp.exp2((s - top) * EXP2_SCALE), 0.0).astype(jnp.bfloat16)
        o = dot_nn(p, jnp.concatenate([dkv_ref[1, h], ones], axis=1))
        total = o[:, HEAD_WIDTH:]
        own_out[here, :] = o[:, :HEAD_WIDTH] / total
        col[here, :] = packed_stats(jnp.broadcast_to(top, total.shape), total)
    own_stats = jnp.transpose(col[...])[0:8]

    for oy in (2, 1, 3, 0):
        for oz in FAR_LAST:
            a_c[oz, oy, 0].wait_recv()
            a_c[oz, oy, 1].wait_recv()
        out, stats = merge(
            [aost[0, oy]] + [ainst[oz, oy] for oz in FAR_LAST],
            [lambda oy=oy: aout[0, oy]]
            + [lambda oz=oz, oy=oy: ain[oz, oy] for oz in FAR_LAST],
        )
        bout[oy] = out.astype(jnp.bfloat16)
        bost[oy] = stats
        if oy:
            for i, (out_ref, into) in enumerate(((bout, bin_), (bost, binst))):
                c = remote(out_ref.at[oy], into.at[oy], b_s.at[oy, i], b_r.at[oy, i], SIDE - oy, 0)
                c.start()
                b_c[oy, i] = c

    for oy in FAR_LAST:
        p_c[oy, 0].wait_recv()
        p_c[oy, 1].wait_recv()
    out, _ = merge(
        [pst[0]] + [pinst[oy] for oy in FAR_LAST],
        [lambda: pout[0]] + [lambda oy=oy: pin[oy] for oy in FAR_LAST],
    )
    out = out.astype(jnp.bfloat16)
    for h in range(KEY_HEADS):
        att_ref[:, pl.ds(h * HEAD_WIDTH, HEAD_WIDTH)] = out[h * rows : (h + 1) * rows]

    for oy in FAR_LAST:
        b_c[oy, 0].wait_recv()
        b_c[oy, 1].wait_recv()
    out, _ = merge(
        [own_stats, bost[0]] + [binst[oy] for oy in FAR_LAST],
        [lambda: own_out[...], lambda: bout[0]] + [lambda oy=oy: bin_[oy] for oy in FAR_LAST],
    )
    dec_ref[...] = out.astype(jnp.bfloat16)

    for copies in (q_c, kv_c, ks_c, d_c, p_c, a_c, b_c):
        for c in copies.values():
            c.wait_send()


def on_device(
    span_queries,
    span_key_value,
    prompt_key_value,
    span_start,
    block_pool_key_value,
    block_dest,
    block_request,
    block_fill,
    decode_query,
    decoded_key_value,
):
    steps, requests = decode_query.shape[:2]
    rows = span_queries.shape[0]
    block = KEY_HEADS * rows
    keys = prompt_key_value.shape[1]
    slots = block_slots(block_dest[:, 0], block_request, block_fill)
    dq = decode_query.reshape(steps, requests, KEY_HEADS, HEAD_GROUP, HEAD_WIDTH)
    dq = dq.transpose(2, 1, 0, 3, 4).reshape(block, HEAD_WIDTH)
    dkv = decoded_key_value.reshape(steps, 2, requests, KEY_HEADS, HEAD_WIDTH)
    dkv = dkv.transpose(1, 3, 2, 0, 4)
    dkv = jnp.pad(dkv, ((0, 0), (0, 0), (0, 0), (0, 8 - steps), (0, 0)))
    dkv = dkv.reshape(2, KEY_HEADS, 8 * requests, HEAD_WIDTH)

    bf, f32 = jnp.bfloat16, jnp.float32
    part = (block, HEAD_WIDTH)
    stat = (8, block)
    vmem = pl.BlockSpec(memory_space=pltpu.VMEM)
    smem = pl.BlockSpec(memory_space=pltpu.SMEM)
    dma = pltpu.SemaphoreType.DMA
    attended, dec = pl.pallas_call(
        fused_kernel,
        out_shape=(
            jax.ShapeDtypeStruct(span_queries.shape, bf),
            jax.ShapeDtypeStruct(part, bf),
        ),
        in_specs=[vmem, vmem, vmem, smem, pl.BlockSpec(memory_space=pl.ANY), smem, vmem, vmem],
        out_specs=(vmem, vmem),
        scratch_shapes=[
            pltpu.VMEM((SIDE,) + part, bf),
            pltpu.VMEM((SIDE, 2, keys, HEAD_WIDTH), bf),
            pltpu.VMEM((2, SIDE * rows, HEAD_WIDTH), bf),
            pltpu.VMEM((keys, 2 * HEAD_WIDTH), bf),
            pltpu.VMEM((SIDE, SIDE) + part, bf),
            pltpu.VMEM(block_pool_key_value.shape, bf),
            pltpu.VMEM((SIDE, block, 2 * HEAD_WIDTH), f32),
            pltpu.VMEM((SIDE,) + part, f32),
            pltpu.VMEM(part, f32),
            pltpu.VMEM((SIDE,) + part, bf),
            pltpu.VMEM((SIDE,) + stat, f32),
            pltpu.VMEM((SIDE,) + part, bf),
            pltpu.VMEM((SIDE,) + stat, f32),
            pltpu.VMEM((SIDE, SIDE) + part, bf),
            pltpu.VMEM((SIDE, SIDE) + stat, f32),
            pltpu.VMEM((SIDE, SIDE) + part, bf),
            pltpu.VMEM((SIDE, SIDE) + stat, f32),
            pltpu.VMEM((SIDE,) + part, bf),
            pltpu.VMEM((SIDE,) + stat, f32),
            pltpu.VMEM((SIDE,) + part, bf),
            pltpu.VMEM((SIDE,) + stat, f32),
            pltpu.VMEM(part, f32),
            dma,
            dma((SIDE,)), dma((SIDE,)),
            dma((SIDE,)), dma((SIDE,)),
            dma((SIDE,)), dma((SIDE,)),
            dma((SIDE, SIDE)), dma((SIDE, SIDE)),
            dma((SIDE, 2)), dma((SIDE, 2)),
            dma((SIDE, SIDE, 2)), dma((SIDE, SIDE, 2)),
            dma((SIDE, 2)), dma((SIDE, 2)),
        ],
        compiler_params=pltpu.CompilerParams(
            collective_id=0, has_side_effects=True, vmem_limit_bytes=48 * 1024 * 1024
        ),
        name="span_and_decode",
    )(span_queries, span_key_value, prompt_key_value, span_start, block_pool_key_value, slots,
      dq, dkv)
    dec = dec.reshape(KEY_HEADS, requests, steps, HEAD_GROUP, HEAD_WIDTH)
    dec = dec.transpose(2, 1, 0, 3, 4).reshape(steps, requests, QUERY_HEADS * HEAD_WIDTH)
    return attended, dec


def solution(mesh):
    placed = (
        P("seq", "req"),
        P(None, "seq", "req"),
        P(None, "seq", "req"),
        P(),
        P(("seq", "req"), None, None, None),
        P(("seq", "req"), None),
        P(("seq", "req")),
        P(("seq", "req")),
        P(None, ("seq", "req"), None),
        P(None, None, ("seq", "req"), None),
    )
    return jax.shard_map(
        on_device,
        mesh=mesh,
        in_specs=placed,
        out_specs=(P("seq", "req"), P(None, ("seq", "req"), None)),
        check_vma=False,
    )
```

```python
import functools

import jax
import jax.numpy as jnp
from jax import lax
from jax.experimental import pallas as pl
from jax.experimental.pallas import tpu as pltpu
from jax.sharding import PartitionSpec as P

QUERY_HEADS = 64
KEY_HEADS = 8
HEAD_WIDTH = 128
HEAD_GROUP = QUERY_HEADS // KEY_HEADS
CAP = 4
SIDE = 4
HOMES = SIDE * SIDE

MASK_NEGATIVE = -1e30
EXP2_SCALE = HEAD_WIDTH ** (-0.5) * 1.4426950408889634
FAR_LAST = (1, 3, 2)
SPAN_CHUNK = 256
Z_ROWS = 384


def dot_nt(a, b):
    return lax.dot_general(a, b, (((1,), (1,)), ((), ())), preferred_element_type=jnp.float32)


def dot_nn(a, b):
    return lax.dot_general(a, b, (((1,), (0,)), ((), ())), preferred_element_type=jnp.float32)


def packed_stats(top, total):
    lane = lax.broadcasted_iota(jnp.int32, top.shape, 1)
    return jnp.where(lane < 4, top, total)


def join(stats):
    tops = [s[0:4] for s in stats]
    top = functools.reduce(jnp.maximum, tops)
    weights = [jnp.exp2((t - top) * EXP2_SCALE) * s[4:8] for t, s in zip(tops, stats)]
    total = functools.reduce(jnp.add, weights)
    inverse = 1.0 / jnp.where(total > 0.0, total, 1.0)
    return [w * inverse for w in weights], top, total


def blend(shares, row, parts):
    out = None
    for share, part in zip(shares, parts):
        wide = jnp.broadcast_to(share[row : row + 1], (HEAD_WIDTH, share.shape[1]))
        term = jnp.transpose(wide) * part().astype(jnp.float32)
        out = term if out is None else out + term
    return out


def fused_kernel(
    sq_ref, skv_ref, pkv_ref, start_ref, pool_ref, dest_ref, request_ref, fill_ref, dq_ref, dkv_ref,
    att_ref, dec_ref,
    stage, stage_q, span, qb, kv, kvs, vv, dqb, dkv, pool, acc, mx, col,
    pout, pst, pin, pinst,
    zout, yout, zst, yst, zin, zinst, yin, yinst,
    zb, zbst, zbin, zbinst, yb, ybst, ybin, ybinst,
    own_out, own_st,
    load_sem, q_s, q_r, kv_s, kv_r, ks_s, ks_r, d_s, d_r, f_s, f_r, p_s, p_r,
    za_s, za_r, zs_s, zs_r, ya_s, ya_r, ys_s, ys_r, zb_s, zb_r, yb_s, yb_r,
):
    me = lax.axis_index("seq")
    y, z = me // SIDE, me % SIDE
    rows = sq_ref.shape[0]
    block = KEY_HEADS * rows
    keys = pkv_ref.shape[1]
    mesh_id = pl.DeviceIdType.MESH
    near = (1, 3)

    def at(dy, dz):
        return {"seq": (y + dy) % SIDE * SIDE + (z + dz) % SIDE}

    def remote(src, dst, send, recv, dy, dz):
        return pltpu.make_async_remote_copy(
            src_ref=src, dst_ref=dst, send_sem=send, recv_sem=recv,
            device_id=at(dy, dz), device_id_type=mesh_id,
        )

    sent = []

    def send(*args):
        copy = remote(*args)
        copy.start()
        sent.append(copy)
        return copy

    barrier = pltpu.get_barrier_semaphore()
    for o in (1, 2, 3):
        pl.semaphore_signal(barrier, inc=1, device_id=at(o, 0), device_id_type=mesh_id)
        pl.semaphore_signal(barrier, inc=1, device_id=at(0, o), device_id_type=mesh_id)

    load_prompt = pltpu.make_async_copy(pkv_ref, stage, load_sem.at[0])
    load_dq = pltpu.make_async_copy(dq_ref, dqb.at[0, 0], load_sem.at[1])
    load_span = pltpu.make_async_copy(skv_ref, span, load_sem.at[2])
    load_pool = pltpu.make_async_copy(pool_ref, pool, load_sem.at[3])
    load_dkv = pltpu.make_async_copy(dkv_ref, dkv, load_sem.at[4])
    load_queries = pltpu.make_async_copy(sq_ref, stage_q, load_sem.at[5])
    load_dq.start()
    load_queries.start()
    for c in (load_prompt, load_span, load_pool, load_dkv):
        c.start()

    load_dq.wait()
    load_queries.wait()
    for h in range(KEY_HEADS):
        qb[0, pl.ds(h * rows, rows), :] = stage_q[:, pl.ds(h * HEAD_WIDTH, HEAD_WIDTH)]
    pl.semaphore_wait(barrier, 6)

    q_c, d_c, f_c, kv_c, ks_c = {}, {}, {}, {}, {}
    for o in FAR_LAST:
        q_c[o] = send(qb.at[0], qb.at[o], q_s.at[o], q_r.at[o], o, 0)
        d_c[0, o] = send(dqb.at[0, 0], dqb.at[0, o], d_s.at[0, o], d_r.at[0, o], 0, o)

    def pass_queries(oz):
        for o in near:
            d_c[o, oz] = send(dqb.at[0, oz], dqb.at[o, oz], d_s.at[o, oz], d_r.at[o, oz], o, 0)

    def pass_queries_on(oz):
        for i, o in enumerate(near):
            d_c[o, oz].wait_recv()
            f_c[oz, i] = send(
                dqb.at[o, oz, i], dqb.at[2, oz, i], f_s.at[oz, i], f_r.at[oz, i], o, 0
            )

    pass_queries(0)

    load_prompt.wait()
    start = start_ref[0]
    position = me * keys + lax.broadcasted_iota(jnp.int32, (keys, HEAD_WIDTH), 0)
    own_keys = stage[0].astype(jnp.float32)
    kv[0, 0] = jnp.where(position < start, own_keys, own_keys[0:1]).astype(jnp.bfloat16)
    kv[0, 1] = jnp.where(position < start, stage[1].astype(jnp.float32), 0.0).astype(jnp.bfloat16)
    for first in (0, 1):
        for i, o in enumerate(near):
            c = (first + i) % 2
            kv_c[o, c] = send(kv.at[0, c], kv.at[o, c], kv_s.at[o, c], kv_r.at[o, c], 0, o)
    load_span.wait()
    kvs[0] = span[...]
    for o in FAR_LAST:
        ks_c[o] = send(
            span, kvs.at[o], ks_s.at[o], ks_r.at[o], 0, o
        )

    def pass_shards_on():
        for c, o in enumerate(near):
            kv_c[o, c].wait_recv()
            kv_c[2, c] = send(kv.at[o, c], kv.at[2, c], kv_s.at[2, c], kv_r.at[2, c], 0, o)

    def load_values(oz):
        shard = y * SIDE + (z - oz + SIDE) % SIDE
        position = shard * keys + lax.broadcasted_iota(jnp.int32, (keys, HEAD_WIDTH), 0)
        vv[:, 0:HEAD_WIDTH] = kv[oz, 1]
        vv[:, HEAD_WIDTH:] = jnp.where(position < start, 1.0, 0.0).astype(jnp.bfloat16)

    def prompt_rows(oy, oz, first):
        s = dot_nt(qb[oy], kv[oz, 0])
        top = jnp.broadcast_to(jnp.max(s, axis=1, keepdims=True), (block, HEAD_WIDTH))
        if not first:
            old = mx[oy]
            top = jnp.maximum(old, top)
        wide = jnp.concatenate([top] * (keys // HEAD_WIDTH), axis=1)
        p = jnp.exp2((s - wide) * EXP2_SCALE).astype(jnp.bfloat16)
        o = dot_nn(p, vv[...])
        if not first:
            keep = jnp.exp2((old - top) * EXP2_SCALE)
            o = o + acc[oy] * jnp.concatenate([keep, keep], axis=1)
        acc[oy] = o
        mx[oy] = top

    def prompt_block(oz):
        def step(i, _):
            prompt_rows(2 * i, oz, False)
            prompt_rows(2 * i + 1, oz, False)
            return 0

        lax.fori_loop(0, SIDE // 2, step, 0)

    def span_block(oy):
        width = SIDE * rows
        ones = jnp.ones((width, HEAD_WIDTH), jnp.bfloat16)
        values = jnp.concatenate([jnp.concatenate([kvs[o, 1] for o in range(SIDE)], axis=0), ones], axis=1)
        span_keys = jnp.concatenate([kvs[o, 0] for o in range(SIDE)], axis=0)
        row_base = ((y - oy + SIDE) % SIDE * SIDE + z) * rows

        def step(i, _):
            here = pl.ds(pl.multiple_of(i * SPAN_CHUNK, SPAN_CHUNK), SPAN_CHUNK)
            s = dot_nt(qb[oy, here, :], span_keys)
            row = row_base + lax.broadcasted_iota(jnp.int32, (SPAN_CHUNK, width), 0) % rows
            key = lax.broadcasted_iota(jnp.int32, (SPAN_CHUNK, width), 1)
            key = (y * SIDE + (z - key // rows + SIDE) % SIDE) * rows + key % rows
            valid = key <= row
            s = jnp.where(valid, s, MASK_NEGATIVE)
            old = mx[oy, here, :]
            top = jnp.broadcast_to(jnp.max(s, axis=1, keepdims=True), (SPAN_CHUNK, HEAD_WIDTH))
            top = jnp.maximum(old, top)
            wide = jnp.concatenate([top] * (width // HEAD_WIDTH), axis=1)
            p = jnp.where(valid, jnp.exp2((s - wide) * EXP2_SCALE), 0.0).astype(jnp.bfloat16)
            o = dot_nn(p, values)
            keep = jnp.exp2((old - top) * EXP2_SCALE)
            o = o + acc[oy, here, :] * jnp.concatenate([keep, keep], axis=1)
            total = o[:, HEAD_WIDTH:]
            pout[oy, here, :] = (o[:, :HEAD_WIDTH] / total).astype(jnp.bfloat16)
            col[here, :] = packed_stats(top, total)
            return 0

        lax.fori_loop(0, block // SPAN_CHUNK, step, 0)
        pst[oy] = jnp.transpose(col[...])[0:8]

    pair_rows = block // KEY_HEADS
    tokens = pool.shape[2]
    window = CAP * tokens

    def slots_of(home):
        def scan(b, carry):
            count, found = carry[0], carry[1:]
            hit = dest_ref[b, 0] == home
            found = [jnp.where(hit & (count == c), b, f) for c, f in enumerate(found)]
            return (count + hit.astype(jnp.int32), *found)

        zero = jnp.int32(0)
        count, *found = lax.fori_loop(0, pool.shape[0], scan, (zero,) * (1 + CAP), unroll=4)
        fills = [jnp.where(count > c, fill_ref[f], 0) for c, f in enumerate(found)]
        return found, [request_ref[f] for f in found], fills

    def query_rows(oy, oz, h):
        half = KEY_HEADS // 2
        return dqb[oy, oz, h // half, pl.ds(h % half * pair_rows, pair_rows), :]

    def decode_home(oy, oz):
        home = (y - oy + SIDE) % SIDE * SIDE + (z - oz + SIDE) % SIDE
        index, requests, fills = slots_of(home)
        row = lax.broadcasted_iota(jnp.int32, (pair_rows, window), 0)
        key = lax.broadcasted_iota(jnp.int32, (pair_rows, window), 1)
        which = key // tokens
        request = jnp.zeros((pair_rows, window), jnp.int32)
        fill = jnp.zeros((pair_rows, window), jnp.int32)
        for c in range(CAP):
            request = jnp.where(which == c, requests[c], request)
            fill = jnp.where(which == c, fills[c], fill)
        valid = (row // (pair_rows // 2) == request) & (key % tokens < fill)
        valid_float = jnp.where(valid, 1.0, 0.0)
        ones = jnp.ones((window, HEAD_WIDTH), jnp.bfloat16)

        for h in range(KEY_HEADS):
            lanes = pl.ds(h * HEAD_WIDTH, HEAD_WIDTH)
            here = pl.ds(h * pair_rows, pair_rows)
            k = jnp.concatenate([pool[i, 0, :, lanes] for i in index], axis=0)
            v = jnp.concatenate([pool[i, 1, :, lanes] for i in index], axis=0)
            ok = valid_float > 0.5
            s = jnp.where(ok, dot_nt(query_rows(oy, oz, h), k), MASK_NEGATIVE)
            top = jnp.max(s, axis=1, keepdims=True)
            p = jnp.where(ok, jnp.exp2((s - top) * EXP2_SCALE), 0.0).astype(jnp.bfloat16)
            o = dot_nn(p, jnp.concatenate([v, ones], axis=1))
            total = o[:, HEAD_WIDTH:]
            out = o[:, :HEAD_WIDTH] / jnp.where(total > 0.0, total, 1.0)
            out = out.astype(jnp.bfloat16)
            if h < Z_ROWS // pair_rows:
                zout[oz, oy, here, :] = out
            else:
                yout[oy, oz, pl.ds(h * pair_rows - Z_ROWS, pair_rows), :] = out
            col[here, :] = packed_stats(jnp.broadcast_to(top, total.shape), total)
        stats = jnp.transpose(col[...])[0:8]
        for i in (0, 4):
            zst[oz, i + oy : i + oy + 1, :] = stats[i + oy : i + oy + 1, :Z_ROWS]
            yst[oy, i + oz : i + oz + 1, :] = stats[i + oz : i + oz + 1, Z_ROWS:]

    za_c, zs_c, ya_c, ys_c = {}, {}, {}, {}
    z_part, y_part = pl.ds(0, Z_ROWS), pl.ds(Z_ROWS, block - Z_ROWS)

    def send_partials(oy, oz):
        if oz:
            za_c[oz, oy] = send(
                zout.at[oz, oy], zin.at[oz, oy], za_s.at[oz, oy], za_r.at[oz, oy],
                0, SIDE - oz,
            )
        if oy:
            ya_c[oy, oz] = send(
                yout.at[oy, oz], yin.at[oy, oz], ya_s.at[oy, oz], ya_r.at[oy, oz],
                SIDE - oy, 0,
            )

    def send_z_stats(oz):
        zs_c[oz] = send(zst.at[oz], zinst.at[oz], zs_s.at[oz], zs_r.at[oz], 0, SIDE - oz)

    def send_y_stats(oy):
        ys_c[oy] = send(yst.at[oy], yinst.at[oy], ys_s.at[oy], ys_r.at[oy], SIDE - oy, 0)

    def home(oy, oz):
        decode_home(oy, oz)
        send_partials(oy, oz)

    load_values(0)
    prompt_rows(0, 0, True)
    for oz in FAR_LAST:
        d_c[0, oz].wait_recv()
        pass_queries(oz)
    for oy in FAR_LAST:
        q_c[oy].wait_recv()
        prompt_rows(oy, 0, True)
    load_pool.wait()
    home(0, 0)
    for oz in FAR_LAST:
        home(0, oz)
    pass_queries_on(0)
    home(1, 0)
    home(3, 0)
    pass_shards_on()
    for oz in FAR_LAST:
        pass_queries_on(oz)
        home(1, oz)
        home(3, oz)
        if oz != 2:
            kv_c[oz, oz // 2 ^ 1].wait_recv()
            load_values(oz)
            prompt_block(oz)
    for oz in (1, 3, 2, 0):
        f_c[oz, 0].wait_recv()
        f_c[oz, 1].wait_recv()
        home(2, oz)
    for o in FAR_LAST:
        send_z_stats(o)
        send_y_stats(o)

    kv_c[2, 0].wait_recv()
    kv_c[2, 1].wait_recv()
    load_values(2)
    prompt_block(2)
    for oz in FAR_LAST:
        ks_c[oz].wait_recv()
    p_c = {}
    for oy in (2, 1, 3, 0):
        span_block(oy)
        if oy:
            p_c[oy, 0] = send(pout.at[oy], pin.at[oy], p_s.at[oy, 0], p_r.at[oy, 0], SIDE - oy, 0)
            p_c[oy, 1] = send(
                pst.at[oy], pinst.at[oy], p_s.at[oy, 1], p_r.at[oy, 1], SIDE - oy, 0
            )

    load_dkv.wait()
    extra = dkv.shape[2]
    row = lax.broadcasted_iota(jnp.int32, (pair_rows, extra), 0)
    key = lax.broadcasted_iota(jnp.int32, (pair_rows, extra), 1)
    step_of_row = row % (pair_rows // 2) // HEAD_GROUP
    fresh = (row // (pair_rows // 2) == key // (extra // 2)) & (key % (extra // 2) <= step_of_row)
    ones = jnp.ones((extra, HEAD_WIDTH), jnp.bfloat16)
    for h in range(KEY_HEADS):
        here = pl.ds(h * pair_rows, pair_rows)
        s = jnp.where(fresh, dot_nt(query_rows(0, 0, h), dkv[0, h]), MASK_NEGATIVE)
        top = jnp.max(s, axis=1, keepdims=True)
        p = jnp.where(fresh, jnp.exp2((s - top) * EXP2_SCALE), 0.0).astype(jnp.bfloat16)
        o = dot_nn(p, jnp.concatenate([dkv[1, h], ones], axis=1))
        total = o[:, HEAD_WIDTH:]
        own_out[here, :] = o[:, :HEAD_WIDTH] / total
        col[here, :] = packed_stats(jnp.broadcast_to(top, total.shape), total)
    own_st[...] = jnp.transpose(col[...])[0:8]

    def spread(top, total, row):
        shape = (8, top.shape[1])
        sub = lax.broadcasted_iota(jnp.int32, shape, 0)
        return jnp.where(
            sub < 4,
            jnp.broadcast_to(top[row : row + 1], shape),
            jnp.broadcast_to(total[row : row + 1], shape),
        )

    zb_c, yb_c = {}, {}
    for oz in FAR_LAST:
        zs_c[oz].wait_recv()
    shares, top, total = join([zst[0]] + [zinst[oz] for oz in FAR_LAST])
    for oy in (1, 3, 2, 0):
        for oz in FAR_LAST:
            za_c[oz, oy].wait_recv()
        out = blend(
            shares, oy,
            [lambda oy=oy: zout[0, oy]]
            + [lambda oz=oz, oy=oy: zin[oz, oy] for oz in FAR_LAST],
        )
        zb[oy] = out.astype(jnp.bfloat16)
        zbst[oy] = spread(top, total, oy)
        if oy:
            zb_c[oy, 0] = send(zb.at[oy], zbin.at[oy], zb_s.at[oy, 0], zb_r.at[oy, 0], SIDE - oy, 0)
            zb_c[oy, 1] = send(
                zbst.at[oy], zbinst.at[oy], zb_s.at[oy, 1], zb_r.at[oy, 1], SIDE - oy, 0
            )
    for oy in FAR_LAST:
        ys_c[oy].wait_recv()
    shares, top, total = join([yst[0]] + [yinst[oy] for oy in FAR_LAST])
    for oz in (1, 3, 2, 0):
        for oy in FAR_LAST:
            ya_c[oy, oz].wait_recv()
        out = blend(
            shares, oz,
            [lambda oz=oz: yout[0, oz]]
            + [lambda oz=oz, oy=oy: yin[oy, oz] for oy in FAR_LAST],
        )
        yb[oz] = out.astype(jnp.bfloat16)
        ybst[oz] = spread(top, total, oz)
        if oz:
            yb_c[oz, 0] = send(yb.at[oz], ybin.at[oz], yb_s.at[oz, 0], yb_r.at[oz, 0], 0, SIDE - oz)
            yb_c[oz, 1] = send(
                ybst.at[oz], ybinst.at[oz], yb_s.at[oz, 1], yb_r.at[oz, 1], 0, SIDE - oz
            )

    for oy in FAR_LAST:
        p_c[oy, 0].wait_recv()
        p_c[oy, 1].wait_recv()
    shares, _, _ = join([pst[0]] + [pinst[oy] for oy in FAR_LAST])
    out = blend(shares, 0, [lambda: pout[0]] + [lambda oy=oy: pin[oy] for oy in FAR_LAST])
    out = out.astype(jnp.bfloat16)
    for h in range(KEY_HEADS):
        att_ref[:, pl.ds(h * HEAD_WIDTH, HEAD_WIDTH)] = out[h * rows : (h + 1) * rows]

    for c in list(zb_c.values()) + list(yb_c.values()):
        c.wait_recv()
    for part, n, part_out, part_st, into, into_st in (
        (z_part, Z_ROWS, zb, zbst, zbin, zbinst),
        (y_part, block - Z_ROWS, yb, ybst, ybin, ybinst),
    ):
        shares, _, _ = join(
            [own_st[:, part], part_st[0]] + [into_st[o] for o in FAR_LAST]
        )
        out = blend(
            shares, 0,
            [lambda part=part: own_out[part, :], lambda part_out=part_out: part_out[0]]
            + [lambda o=o, into=into: into[o] for o in FAR_LAST],
        )
        dec_ref[part, :] = out.astype(jnp.bfloat16)

    for c in sent:
        c.wait_send()


def on_device(
    span_queries,
    span_key_value,
    prompt_key_value,
    span_start,
    block_pool_key_value,
    block_dest,
    block_request,
    block_fill,
    decode_query,
    decoded_key_value,
):
    steps, requests = decode_query.shape[:2]
    rows = span_queries.shape[0]
    block = KEY_HEADS * rows
    keys = prompt_key_value.shape[1]
    dq = decode_query.reshape(steps, requests, KEY_HEADS, HEAD_GROUP, HEAD_WIDTH)
    dq = dq.transpose(2, 1, 0, 3, 4).reshape(2, block // 2, HEAD_WIDTH)
    dkv = decoded_key_value.reshape(steps, 2, requests, KEY_HEADS, HEAD_WIDTH)
    dkv = dkv.transpose(1, 3, 2, 0, 4)
    dkv = jnp.pad(dkv, ((0, 0), (0, 0), (0, 0), (0, 8 - steps), (0, 0)))
    dkv = dkv.reshape(2, KEY_HEADS, 8 * requests, HEAD_WIDTH)

    bf, f32 = jnp.bfloat16, jnp.float32
    part = (block, HEAD_WIDTH)
    z_part, y_part = (Z_ROWS, HEAD_WIDTH), (block - Z_ROWS, HEAD_WIDTH)
    stat, z_stat, y_stat = (8, block), (8, Z_ROWS), (8, block - Z_ROWS)
    vmem = pl.BlockSpec(memory_space=pltpu.VMEM)
    smem = pl.BlockSpec(memory_space=pltpu.SMEM)
    hbm = pl.BlockSpec(memory_space=pl.ANY)
    dma = pltpu.SemaphoreType.DMA
    one, two = (SIDE,), (SIDE, SIDE)
    buffers = [
        ((2, keys, HEAD_WIDTH), bf),
        (span_queries.shape, bf),
        ((2, rows, HEAD_WIDTH), bf),
        (one + part, bf),
        ((SIDE, 2, keys, HEAD_WIDTH), bf),
        ((SIDE, 2, rows, HEAD_WIDTH), bf),
        ((keys, 2 * HEAD_WIDTH), bf),
        (two + dq.shape, bf),
        (dkv.shape, bf),
        (block_pool_key_value.shape, bf),
        ((SIDE, block, 2 * HEAD_WIDTH), f32),
        (one + part, f32),
        (part, f32),
        (one + part, bf), (one + stat, f32),
        (one + part, bf), (one + stat, f32),
        (two + z_part, bf), (two + y_part, bf),
        (one + z_stat, f32), (one + y_stat, f32),
        (two + z_part, bf), (one + z_stat, f32),
        (two + y_part, bf), (one + y_stat, f32),
        (one + z_part, bf), (one + z_stat, f32),
        (one + z_part, bf), (one + z_stat, f32),
        (one + y_part, bf), (one + y_stat, f32),
        (one + y_part, bf), (one + y_stat, f32),
        (part, f32), (stat, f32),
    ]
    pairs = [one, (SIDE, 2), one, two, (SIDE, 2), (SIDE, 2), two, one, two, one, (SIDE, 2), (SIDE, 2)]
    semaphores = [dma((6,))]
    for shape in pairs:
        semaphores += [dma(shape), dma(shape)]
    attended, dec = pl.pallas_call(
        fused_kernel,
        out_shape=(
            jax.ShapeDtypeStruct(span_queries.shape, bf),
            jax.ShapeDtypeStruct(part, bf),
        ),
        in_specs=[hbm, hbm, hbm, smem, hbm, smem, smem, smem, hbm, hbm],
        out_specs=(vmem, vmem),
        scratch_shapes=[pltpu.VMEM(shape, dtype) for shape, dtype in buffers] + semaphores,
        compiler_params=pltpu.CompilerParams(
            collective_id=0, has_side_effects=True, vmem_limit_bytes=48 * 1024 * 1024
        ),
        name="span_and_decode",
    )(span_queries, span_key_value, prompt_key_value, span_start, block_pool_key_value, block_dest,
      block_request, block_fill, dq, dkv)
    dec = dec.reshape(KEY_HEADS, requests, steps, HEAD_GROUP, HEAD_WIDTH)
    dec = dec.transpose(2, 1, 0, 3, 4).reshape(steps, requests, QUERY_HEADS * HEAD_WIDTH)
    return attended, dec


def solution(mesh):
    placed = (
        P("seq", "req"),
        P(None, "seq", "req"),
        P(None, "seq", "req"),
        P(),
        P(("seq", "req"), None, None, None),
        P(("seq", "req"), None),
        P(("seq", "req")),
        P(("seq", "req")),
        P(None, ("seq", "req"), None),
        P(None, None, ("seq", "req"), None),
    )
    return jax.shard_map(
        on_device,
        mesh=mesh,
        in_specs=placed,
        out_specs=(P("seq", "req"), P(None, ("seq", "req"), None)),
        check_vma=False,
    )
```

```python
import functools

import jax
import jax.numpy as jnp
from jax import lax
from jax.experimental import pallas as pl
from jax.experimental.pallas import tpu as pltpu
from jax.sharding import PartitionSpec as P

QUERY_HEADS = 64
KEY_HEADS = 8
HEAD_WIDTH = 128
HEAD_GROUP = QUERY_HEADS // KEY_HEADS
CAP = 4
SIDE = 4
HOMES = SIDE * SIDE

MASK_NEGATIVE = -1e30
EXP2_SCALE = HEAD_WIDTH ** (-0.5) * 1.4426950408889634
FAR_LAST = (1, 3, 2)
SPAN_CHUNK = 256
Z_ROWS = 384


def dot_nt(a, b):
    return lax.dot_general(a, b, (((1,), (1,)), ((), ())), preferred_element_type=jnp.float32)


def dot_nn(a, b):
    return lax.dot_general(a, b, (((1,), (0,)), ((), ())), preferred_element_type=jnp.float32)


def packed_stats(top, total):
    lane = lax.broadcasted_iota(jnp.int32, top.shape, 1)
    return jnp.where(lane < 4, top, total)


def join(stats):
    tops = [s[0:4] for s in stats]
    top = functools.reduce(jnp.maximum, tops)
    weights = [jnp.exp2((t - top) * EXP2_SCALE) * s[4:8] for t, s in zip(tops, stats)]
    total = functools.reduce(jnp.add, weights)
    inverse = 1.0 / jnp.where(total > 0.0, total, 1.0)
    return [w * inverse for w in weights], top, total


def blend(shares, row, parts):
    out = None
    for share, part in zip(shares, parts):
        wide = jnp.broadcast_to(share[row : row + 1], (HEAD_WIDTH, share.shape[1]))
        term = jnp.transpose(wide) * part().astype(jnp.float32)
        out = term if out is None else out + term
    return out


def fused_kernel(
    sq_ref, skv_ref, pkv_ref, start_ref, pool_ref, dest_ref, request_ref, fill_ref, dq_ref, dkv_ref,
    att_ref, dec_ref,
    stage, stage_q, span, qb, kv, kvs, vv, dqb, stage_d, dkv, pool, acc, mx, col,
    pout, pst, pin, pinst,
    zout, yout, zst, yst, zin, zinst, yin, yinst,
    zb, zbst, zbin, zbinst, yb, ybst, ybin, ybinst,
    own_out, own_st,
    load_sem, q_s, q_r, kv_s, kv_r, ks_s, ks_r, d_s, d_r, f_s, f_r, p_s, p_r,
    za_s, za_r, zs_s, zs_r, ya_s, ya_r, ys_s, ys_r, zb_s, zb_r, yb_s, yb_r,
):
    me = lax.axis_index("seq")
    y, z = me // SIDE, me % SIDE
    rows = sq_ref.shape[0]
    block = KEY_HEADS * rows
    keys = pkv_ref.shape[1]
    mesh_id = pl.DeviceIdType.MESH
    near = (1, 3)

    def at(dy, dz):
        return {"seq": (y + dy) % SIDE * SIDE + (z + dz) % SIDE}

    def remote(src, dst, send, recv, dy, dz):
        return pltpu.make_async_remote_copy(
            src_ref=src, dst_ref=dst, send_sem=send, recv_sem=recv,
            device_id=at(dy, dz), device_id_type=mesh_id,
        )

    sent = []

    def send(*args):
        copy = remote(*args)
        copy.start()
        sent.append(copy)
        return copy

    barrier = pltpu.get_barrier_semaphore()
    for o in (1, 2, 3):
        pl.semaphore_signal(barrier, inc=1, device_id=at(o, 0), device_id_type=mesh_id)
        pl.semaphore_signal(barrier, inc=1, device_id=at(0, o), device_id_type=mesh_id)

    load_prompt = pltpu.make_async_copy(pkv_ref, stage, load_sem.at[0])
    load_dq = pltpu.make_async_copy(dq_ref, dqb.at[0, 0], load_sem.at[1])
    load_span = pltpu.make_async_copy(skv_ref, span, load_sem.at[2])
    load_pool = pltpu.make_async_copy(pool_ref, pool, load_sem.at[3])
    load_dkv = pltpu.make_async_copy(dkv_ref, stage_d, load_sem.at[4])
    load_queries = pltpu.make_async_copy(sq_ref, stage_q, load_sem.at[5])
    load_dq.start()
    load_queries.start()
    for c in (load_prompt, load_span, load_pool, load_dkv):
        c.start()

    load_dq.wait()
    load_queries.wait()
    for h in range(KEY_HEADS):
        qb[0, h // 4, pl.ds(h % 4 * rows, rows), :] = stage_q[:, pl.ds(h * HEAD_WIDTH, HEAD_WIDTH)]
    pl.semaphore_wait(barrier, 6)

    q_c, d_c, f_c, kv_c, ks_c = {}, {}, {}, {}, {}
    for o in FAR_LAST:
        q_c[o] = send(qb.at[0], qb.at[o], q_s.at[o], q_r.at[o], o, 0)
        d_c[0, o] = send(dqb.at[0, 0], dqb.at[0, o], d_s.at[0, o], d_r.at[0, o], 0, o)

    def pass_queries(oz):
        for o in near:
            d_c[o, oz] = send(dqb.at[0, oz], dqb.at[o, oz], d_s.at[o, oz], d_r.at[o, oz], o, 0)

    def pass_queries_on(oz):
        for i, o in enumerate(near):
            d_c[o, oz].wait_recv()
            f_c[oz, i] = send(
                dqb.at[o, oz, i], dqb.at[2, oz, i], f_s.at[oz, i], f_r.at[oz, i], o, 0
            )

    pass_queries(0)

    load_prompt.wait()
    start = start_ref[0]
    position = me * keys + lax.broadcasted_iota(jnp.int32, (keys, HEAD_WIDTH), 0)
    own_keys = stage[0].astype(jnp.float32)
    kv[0, 0] = jnp.where(position < start, own_keys, own_keys[0:1]).astype(jnp.bfloat16)
    kv[0, 1] = jnp.where(position < start, stage[1].astype(jnp.float32), 0.0).astype(jnp.bfloat16)
    for first in (0, 1):
        for i, o in enumerate(near):
            c = (first + i) % 2
            kv_c[o, c] = send(kv.at[0, c], kv.at[o, c], kv_s.at[o, c], kv_r.at[o, c], 0, o)
    load_span.wait()
    kvs[0] = span[...]
    for o in FAR_LAST:
        ks_c[o] = send(
            span, kvs.at[o], ks_s.at[o], ks_r.at[o], 0, o
        )

    def pass_shards_on():
        for c, o in enumerate(near):
            kv_c[o, c].wait_recv()
            kv_c[2, c] = send(kv.at[o, c], kv.at[2, c], kv_s.at[2, c], kv_r.at[2, c], 0, o)

    def load_values(oz):
        shard = y * SIDE + (z - oz + SIDE) % SIDE
        position = shard * keys + lax.broadcasted_iota(jnp.int32, (keys, HEAD_WIDTH), 0)
        vv[:, 0:HEAD_WIDTH] = kv[oz, 1]
        vv[:, HEAD_WIDTH:] = jnp.where(position < start, 1.0, 0.0).astype(jnp.bfloat16)

    def prompt_rows(oy, oz, first):
        s = dot_nt(qb[oy].reshape(block, HEAD_WIDTH), kv[oz, 0])
        top = jnp.broadcast_to(jnp.max(s, axis=1, keepdims=True), (block, HEAD_WIDTH))
        if not first:
            old = mx[oy]
            top = jnp.maximum(old, top)
        wide = jnp.concatenate([top] * (keys // HEAD_WIDTH), axis=1)
        p = jnp.exp2((s - wide) * EXP2_SCALE).astype(jnp.bfloat16)
        o = dot_nn(p, vv[...])
        if not first:
            keep = jnp.exp2((old - top) * EXP2_SCALE)
            o = o + acc[oy] * jnp.concatenate([keep, keep], axis=1)
        acc[oy] = o
        mx[oy] = top

    def prompt_block(oz):
        def step(i, _):
            prompt_rows(2 * i, oz, False)
            prompt_rows(2 * i + 1, oz, False)
            return 0

        lax.fori_loop(0, SIDE // 2, step, 0)

    def span_block(oy):
        width = SIDE * rows
        ones = jnp.ones((width, HEAD_WIDTH), jnp.bfloat16)
        values = jnp.concatenate([jnp.concatenate([kvs[o, 1] for o in range(SIDE)], axis=0), ones], axis=1)
        span_keys = jnp.concatenate([kvs[o, 0] for o in range(SIDE)], axis=0)
        row_base = ((y - oy + SIDE) % SIDE * SIDE + z) * rows

        def step(i, _):
            here = pl.ds(pl.multiple_of(i * SPAN_CHUNK, SPAN_CHUNK), SPAN_CHUNK)
            s = dot_nt(qb[oy, i], span_keys)
            row = row_base + lax.broadcasted_iota(jnp.int32, (SPAN_CHUNK, width), 0) % rows
            key = lax.broadcasted_iota(jnp.int32, (SPAN_CHUNK, width), 1)
            key = (y * SIDE + (z - key // rows + SIDE) % SIDE) * rows + key % rows
            valid = key <= row
            s = jnp.where(valid, s, MASK_NEGATIVE)
            old = mx[oy, here, :]
            top = jnp.broadcast_to(jnp.max(s, axis=1, keepdims=True), (SPAN_CHUNK, HEAD_WIDTH))
            top = jnp.maximum(old, top)
            wide = jnp.concatenate([top] * (width // HEAD_WIDTH), axis=1)
            p = jnp.where(valid, jnp.exp2((s - wide) * EXP2_SCALE), 0.0).astype(jnp.bfloat16)
            o = dot_nn(p, values)
            keep = jnp.exp2((old - top) * EXP2_SCALE)
            o = o + acc[oy, here, :] * jnp.concatenate([keep, keep], axis=1)
            total = o[:, HEAD_WIDTH:]
            pout[oy, here, :] = (o[:, :HEAD_WIDTH] / total).astype(jnp.bfloat16)
            col[here, :] = packed_stats(top, total)
            return 0

        lax.fori_loop(0, block // SPAN_CHUNK, step, 0)
        pst[oy] = jnp.transpose(col[...])[0:8]

    pair_rows = block // KEY_HEADS
    tokens = pool.shape[2]
    window = CAP * tokens

    def slots_of(home):
        def scan(b, carry):
            count, found = carry[0], carry[1:]
            hit = dest_ref[b] == home
            found = [jnp.where(hit & (count == c), b, f) for c, f in enumerate(found)]
            return (count + hit.astype(jnp.int32), *found)

        zero = jnp.int32(0)
        count, *found = lax.fori_loop(0, pool.shape[0], scan, (zero,) * (1 + CAP), unroll=4)
        fills = [jnp.where(count > c, fill_ref[f], 0) for c, f in enumerate(found)]
        return found, [request_ref[f] for f in found], fills

    def query_rows(oy, oz, h):
        half = KEY_HEADS // 2
        return dqb[oy, oz, h // half, pl.ds(h % half * pair_rows, pair_rows), :]

    def decode_home(oy, oz):
        home = (y - oy + SIDE) % SIDE * SIDE + (z - oz + SIDE) % SIDE
        index, requests, fills = slots_of(home)
        row = lax.broadcasted_iota(jnp.int32, (pair_rows, window), 0)
        key = lax.broadcasted_iota(jnp.int32, (pair_rows, window), 1)
        which = key // tokens
        request = jnp.zeros((pair_rows, window), jnp.int32)
        fill = jnp.zeros((pair_rows, window), jnp.int32)
        for c in range(CAP):
            request = jnp.where(which == c, requests[c], request)
            fill = jnp.where(which == c, fills[c], fill)
        valid = (row // (pair_rows // 2) == request) & (key % tokens < fill)
        valid_float = jnp.where(valid, 1.0, 0.0)
        ones = jnp.ones((window, HEAD_WIDTH), jnp.bfloat16)

        for h in range(KEY_HEADS):
            lanes = pl.ds(h * HEAD_WIDTH, HEAD_WIDTH)
            here = pl.ds(h * pair_rows, pair_rows)
            k = jnp.concatenate([pool[i, 0, :, lanes] for i in index], axis=0)
            v = jnp.concatenate([pool[i, 1, :, lanes] for i in index], axis=0)
            ok = valid_float > 0.5
            s = jnp.where(ok, dot_nt(query_rows(oy, oz, h), k), MASK_NEGATIVE)
            top = jnp.max(s, axis=1, keepdims=True)
            p = jnp.where(ok, jnp.exp2((s - top) * EXP2_SCALE), 0.0).astype(jnp.bfloat16)
            o = dot_nn(p, jnp.concatenate([v, ones], axis=1))
            total = o[:, HEAD_WIDTH:]
            out = o[:, :HEAD_WIDTH] / jnp.where(total > 0.0, total, 1.0)
            out = out.astype(jnp.bfloat16)
            if h < Z_ROWS // pair_rows:
                zout[oz, oy, here, :] = out
            else:
                yout[oy, oz, pl.ds(h * pair_rows - Z_ROWS, pair_rows), :] = out
            col[here, :] = packed_stats(jnp.broadcast_to(top, total.shape), total)
        stats = jnp.transpose(col[...])[0:8]
        for i in (0, 4):
            zst[oz, i + oy : i + oy + 1, :] = stats[i + oy : i + oy + 1, :Z_ROWS]
            yst[oy, i + oz : i + oz + 1, :] = stats[i + oz : i + oz + 1, Z_ROWS:]

    za_c, zs_c, ya_c, ys_c = {}, {}, {}, {}
    z_part, y_part = pl.ds(0, Z_ROWS), pl.ds(Z_ROWS, block - Z_ROWS)

    def send_partials(oy, oz):
        if oz:
            za_c[oz, oy] = send(
                zout.at[oz, oy], zin.at[oz, oy], za_s.at[oz, oy], za_r.at[oz, oy],
                0, SIDE - oz,
            )
        if oy:
            ya_c[oy, oz] = send(
                yout.at[oy, oz], yin.at[oy, oz], ya_s.at[oy, oz], ya_r.at[oy, oz],
                SIDE - oy, 0,
            )

    def send_z_stats(oz):
        zs_c[oz] = send(zst.at[oz], zinst.at[oz], zs_s.at[oz], zs_r.at[oz], 0, SIDE - oz)

    def send_y_stats(oy):
        ys_c[oy] = send(yst.at[oy], yinst.at[oy], ys_s.at[oy], ys_r.at[oy], SIDE - oy, 0)

    def home(oy, oz):
        decode_home(oy, oz)
        send_partials(oy, oz)

    load_values(0)
    prompt_rows(0, 0, True)
    for oz in FAR_LAST:
        d_c[0, oz].wait_recv()
        pass_queries(oz)
    for oy in FAR_LAST:
        q_c[oy].wait_recv()
        prompt_rows(oy, 0, True)
    load_pool.wait()
    home(0, 0)
    for oz in FAR_LAST:
        home(0, oz)
    pass_queries_on(0)
    home(1, 0)
    home(3, 0)
    pass_shards_on()
    for oz in FAR_LAST:
        pass_queries_on(oz)
        home(1, oz)
        home(3, oz)
        if oz != 2:
            kv_c[oz, oz // 2 ^ 1].wait_recv()
            load_values(oz)
            prompt_block(oz)
    for oz in (1, 3, 2, 0):
        f_c[oz, 0].wait_recv()
        f_c[oz, 1].wait_recv()
        home(2, oz)
    for o in FAR_LAST:
        send_z_stats(o)
        send_y_stats(o)

    kv_c[2, 0].wait_recv()
    kv_c[2, 1].wait_recv()
    load_values(2)
    prompt_block(2)
    for oz in FAR_LAST:
        ks_c[oz].wait_recv()
    p_c = {}
    for oy in (2, 1, 3, 0):
        span_block(oy)
        if oy:
            p_c[oy, 0] = send(pout.at[oy], pin.at[oy], p_s.at[oy, 0], p_r.at[oy, 0], SIDE - oy, 0)
            p_c[oy, 1] = send(
                pst.at[oy], pinst.at[oy], p_s.at[oy, 1], p_r.at[oy, 1], SIDE - oy, 0
            )

    load_dkv.wait()
    steps, _, requests, _ = stage_d.shape
    dkv[...] = jnp.zeros_like(dkv)
    for u in range(steps):
        for c in range(2):
            new = stage_d[u, c].astype(jnp.float32)
            for h in range(KEY_HEADS):
                dkv[c, h, pl.ds(u * requests, requests), :] = new[
                    :, h * HEAD_WIDTH : (h + 1) * HEAD_WIDTH
                ]
    extra = dkv.shape[2]
    row = lax.broadcasted_iota(jnp.int32, (pair_rows, extra), 0)
    key = lax.broadcasted_iota(jnp.int32, (pair_rows, extra), 1)
    step_of_row = row % (pair_rows // 2) // HEAD_GROUP
    fresh = (row // (pair_rows // 2) == key % requests) & (key // requests <= step_of_row)
    ones = jnp.ones((extra, HEAD_WIDTH), jnp.bfloat16)
    for h in range(KEY_HEADS):
        here = pl.ds(h * pair_rows, pair_rows)
        s = jnp.where(fresh, dot_nt(query_rows(0, 0, h), dkv[0, h].astype(jnp.bfloat16)), MASK_NEGATIVE)
        top = jnp.max(s, axis=1, keepdims=True)
        p = jnp.where(fresh, jnp.exp2((s - top) * EXP2_SCALE), 0.0).astype(jnp.bfloat16)
        o = dot_nn(p, jnp.concatenate([dkv[1, h].astype(jnp.bfloat16), ones], axis=1))
        total = o[:, HEAD_WIDTH:]
        own_out[here, :] = o[:, :HEAD_WIDTH] / total
        col[here, :] = packed_stats(jnp.broadcast_to(top, total.shape), total)
    own_st[...] = jnp.transpose(col[...])[0:8]

    def spread(top, total, row):
        shape = (8, top.shape[1])
        sub = lax.broadcasted_iota(jnp.int32, shape, 0)
        return jnp.where(
            sub < 4,
            jnp.broadcast_to(top[row : row + 1], shape),
            jnp.broadcast_to(total[row : row + 1], shape),
        )

    zb_c, yb_c = {}, {}
    for oz in FAR_LAST:
        zs_c[oz].wait_recv()
    shares, top, total = join([zst[0]] + [zinst[oz] for oz in FAR_LAST])
    for oy in (1, 3, 2, 0):
        for oz in FAR_LAST:
            za_c[oz, oy].wait_recv()
        out = blend(
            shares, oy,
            [lambda oy=oy: zout[0, oy]]
            + [lambda oz=oz, oy=oy: zin[oz, oy] for oz in FAR_LAST],
        )
        zb[oy] = out.astype(jnp.bfloat16)
        zbst[oy] = spread(top, total, oy)
        if oy:
            zb_c[oy, 0] = send(zb.at[oy], zbin.at[oy], zb_s.at[oy, 0], zb_r.at[oy, 0], SIDE - oy, 0)
            zb_c[oy, 1] = send(
                zbst.at[oy], zbinst.at[oy], zb_s.at[oy, 1], zb_r.at[oy, 1], SIDE - oy, 0
            )
    for oy in FAR_LAST:
        ys_c[oy].wait_recv()
    shares, top, total = join([yst[0]] + [yinst[oy] for oy in FAR_LAST])
    for oz in (1, 3, 2, 0):
        for oy in FAR_LAST:
            ya_c[oy, oz].wait_recv()
        out = blend(
            shares, oz,
            [lambda oz=oz: yout[0, oz]]
            + [lambda oz=oz, oy=oy: yin[oy, oz] for oy in FAR_LAST],
        )
        yb[oz] = out.astype(jnp.bfloat16)
        ybst[oz] = spread(top, total, oz)
        if oz:
            yb_c[oz, 0] = send(yb.at[oz], ybin.at[oz], yb_s.at[oz, 0], yb_r.at[oz, 0], 0, SIDE - oz)
            yb_c[oz, 1] = send(
                ybst.at[oz], ybinst.at[oz], yb_s.at[oz, 1], yb_r.at[oz, 1], 0, SIDE - oz
            )

    for oy in FAR_LAST:
        p_c[oy, 0].wait_recv()
        p_c[oy, 1].wait_recv()
    shares, _, _ = join([pst[0]] + [pinst[oy] for oy in FAR_LAST])
    out = blend(shares, 0, [lambda: pout[0]] + [lambda oy=oy: pin[oy] for oy in FAR_LAST])
    out = out.astype(jnp.bfloat16)
    for h in range(KEY_HEADS):
        att_ref[:, pl.ds(h * HEAD_WIDTH, HEAD_WIDTH)] = out[h * rows : (h + 1) * rows]

    for c in list(zb_c.values()) + list(yb_c.values()):
        c.wait_recv()
    for part, n, part_out, part_st, into, into_st in (
        (z_part, Z_ROWS, zb, zbst, zbin, zbinst),
        (y_part, block - Z_ROWS, yb, ybst, ybin, ybinst),
    ):
        shares, _, _ = join(
            [own_st[:, part], part_st[0]] + [into_st[o] for o in FAR_LAST]
        )
        out = blend(
            shares, 0,
            [lambda part=part: own_out[part, :], lambda part_out=part_out: part_out[0]]
            + [lambda o=o, into=into: into[o] for o in FAR_LAST],
        )
        dec_ref[part, :] = out.astype(jnp.bfloat16)

    for c in sent:
        c.wait_send()


def on_device(
    span_queries,
    span_key_value,
    prompt_key_value,
    span_start,
    block_pool_key_value,
    block_dest,
    block_request,
    block_fill,
    decode_query,
    decoded_key_value,
):
    steps, requests = decode_query.shape[:2]
    rows = span_queries.shape[0]
    block = KEY_HEADS * rows
    keys = prompt_key_value.shape[1]
    dq = decode_query.reshape(steps, requests, KEY_HEADS, HEAD_GROUP, HEAD_WIDTH)
    dq = dq.transpose(2, 1, 0, 3, 4).reshape(2, block // 2, HEAD_WIDTH)
    decoded = decoded_key_value.shape

    bf, f32 = jnp.bfloat16, jnp.float32
    part = (block, HEAD_WIDTH)
    z_part, y_part = (Z_ROWS, HEAD_WIDTH), (block - Z_ROWS, HEAD_WIDTH)
    stat, z_stat, y_stat = (8, block), (8, Z_ROWS), (8, block - Z_ROWS)
    vmem = pl.BlockSpec(memory_space=pltpu.VMEM)
    smem = pl.BlockSpec(memory_space=pltpu.SMEM)
    hbm = pl.BlockSpec(memory_space=pltpu.HBM)
    dma = pltpu.SemaphoreType.DMA
    one, two = (SIDE,), (SIDE, SIDE)
    buffers = [
        ((2, keys, HEAD_WIDTH), bf),
        (span_queries.shape, bf),
        ((2, rows, HEAD_WIDTH), bf),
        (one + dq.shape, bf),
        ((SIDE, 2, keys, HEAD_WIDTH), bf),
        ((SIDE, 2, rows, HEAD_WIDTH), bf),
        ((keys, 2 * HEAD_WIDTH), bf),
        (two + dq.shape, bf),
        (decoded, bf), ((2, KEY_HEADS, 2 * steps * requests, HEAD_WIDTH), f32),
        (block_pool_key_value.shape, bf),
        ((SIDE, block, 2 * HEAD_WIDTH), f32),
        (one + part, f32),
        (part, f32),
        (one + part, bf), (one + stat, f32),
        (one + part, bf), (one + stat, f32),
        (two + z_part, bf), (two + y_part, bf),
        (one + z_stat, f32), (one + y_stat, f32),
        (two + z_part, bf), (one + z_stat, f32),
        (two + y_part, bf), (one + y_stat, f32),
        (one + z_part, bf), (one + z_stat, f32),
        (one + z_part, bf), (one + z_stat, f32),
        (one + y_part, bf), (one + y_stat, f32),
        (one + y_part, bf), (one + y_stat, f32),
        (part, f32), (stat, f32),
    ]
    pairs = [one, (SIDE, 2), one, two, (SIDE, 2), (SIDE, 2), two, one, two, one, (SIDE, 2), (SIDE, 2)]
    semaphores = [dma((6,))]
    for shape in pairs:
        semaphores += [dma(shape), dma(shape)]
    attended, dec = pl.pallas_call(
        fused_kernel,
        out_shape=(
            jax.ShapeDtypeStruct(span_queries.shape, bf),
            jax.ShapeDtypeStruct(part, bf),
        ),
        in_specs=[hbm, hbm, hbm, smem, hbm, smem, smem, smem, hbm, hbm],
        out_specs=(vmem, vmem),
        scratch_shapes=[pltpu.VMEM(shape, dtype) for shape, dtype in buffers] + semaphores,
        compiler_params=pltpu.CompilerParams(
            collective_id=0, has_side_effects=True, vmem_limit_bytes=64 * 1024 * 1024 - 65536
        ),
        name="span_and_decode",
    )(span_queries, span_key_value, prompt_key_value, span_start, block_pool_key_value, block_dest[:, 0],
      block_request, block_fill, dq, decoded_key_value)
    dec = dec.reshape(KEY_HEADS, requests, steps, HEAD_GROUP, HEAD_WIDTH)
    dec = dec.transpose(2, 1, 0, 3, 4).reshape(steps, requests, QUERY_HEADS * HEAD_WIDTH)
    return attended, dec


def solution(mesh):
    placed = (
        P("seq", "req"),
        P(None, "seq", "req"),
        P(None, "seq", "req"),
        P(),
        P(("seq", "req"), None, None, None),
        P(("seq", "req"), None),
        P(("seq", "req")),
        P(("seq", "req")),
        P(None, ("seq", "req"), None),
        P(None, None, ("seq", "req"), None),
    )
    return jax.shard_map(
        on_device,
        mesh=mesh,
        in_specs=placed,
        out_specs=(P("seq", "req"), P(None, ("seq", "req"), None)),
        check_vma=False,
    )
```

```python
import functools

import jax
import jax.numpy as jnp
from jax import lax
from jax.experimental import pallas as pl
from jax.experimental.pallas import tpu as pltpu
from jax.sharding import PartitionSpec as P

QUERY_HEADS = 64
KEY_HEADS = 8
HEAD_WIDTH = 128
HEAD_GROUP = QUERY_HEADS // KEY_HEADS
CAP = 4
SIDE = 4
HOMES = SIDE * SIDE

MASK_NEGATIVE = -1e30
EXP2_SCALE = HEAD_WIDTH ** (-0.5) * 1.4426950408889634
FAR_LAST = (1, 3, 2)
SPAN_CHUNK = 256
Z_ROWS = 384


def dot_nt(a, b):
    return lax.dot_general(a, b, (((1,), (1,)), ((), ())), preferred_element_type=jnp.float32)


def dot_nn(a, b):
    return lax.dot_general(a, b, (((1,), (0,)), ((), ())), preferred_element_type=jnp.float32)


def packed_stats(top, total):
    lane = lax.broadcasted_iota(jnp.int32, top.shape, 1)
    return jnp.where(lane < 4, top, total)


def join(stats):
    tops = [s[0:4] for s in stats]
    top = functools.reduce(jnp.maximum, tops)
    weights = [jnp.exp2((t - top) * EXP2_SCALE) * s[4:8] for t, s in zip(tops, stats)]
    total = functools.reduce(jnp.add, weights)
    inverse = 1.0 / jnp.where(total > 0.0, total, 1.0)
    return [w * inverse for w in weights], top, total


def blend(shares, row, parts):
    out = None
    for share, part in zip(shares, parts):
        wide = jnp.broadcast_to(share[row : row + 1], (HEAD_WIDTH, share.shape[1]))
        term = jnp.transpose(wide) * part().astype(jnp.float32)
        out = term if out is None else out + term
    return out


def fused_kernel(
    sq_ref, skv_ref, pkv_ref, start_ref, pool_ref, dest_ref, request_ref, fill_ref, dq_ref, dkv_ref,
    att_ref, dec_ref,
    stage, stage_q, span, qb, kv, kvs, vv, dqb, stage_d, stage_dq, dkv, pool, acc, mx, col,
    pout, pst, pin, pinst,
    zout, yout, zst, zfst, yst, zin, zinst, zfinst, yin, yinst,
    zb, zbst, zbin, zbinst, yb, ybst, ybin, ybinst,
    own_out, own_st, perm,
    load_sem, q_s, q_r, kv_s, kv_r, ks_s, ks_r, d_s, d_r, f_s, f_r, p_s, p_r,
    za_s, za_r, zs_s, zs_r, zf_s, zf_r, ya_s, ya_r, ys_s, ys_r, zb_s, zb_r, yb_s, yb_r,
):
    me = lax.axis_index("seq")
    y, z = me // SIDE, me % SIDE
    rows = sq_ref.shape[0]
    block = KEY_HEADS * rows
    keys = pkv_ref.shape[1]
    mesh_id = pl.DeviceIdType.MESH
    near = (1, 3)

    def at(dy, dz):
        return {"seq": (y + dy) % SIDE * SIDE + (z + dz) % SIDE}

    def remote(src, dst, send, recv, dy, dz):
        return pltpu.make_async_remote_copy(
            src_ref=src, dst_ref=dst, send_sem=send, recv_sem=recv,
            device_id=at(dy, dz), device_id_type=mesh_id,
        )

    sent = []

    def send(*args):
        copy = remote(*args)
        copy.start()
        sent.append(copy)
        return copy

    barrier = pltpu.get_barrier_semaphore()
    for o in (1, 2, 3):
        pl.semaphore_signal(barrier, inc=1, device_id=at(o, 0), device_id_type=mesh_id)
        pl.semaphore_signal(barrier, inc=1, device_id=at(0, o), device_id_type=mesh_id)

    load_prompt = pltpu.make_async_copy(pkv_ref, stage, load_sem.at[0])
    load_dq = pltpu.make_async_copy(dq_ref, stage_dq, load_sem.at[1])
    load_span = pltpu.make_async_copy(skv_ref, span, load_sem.at[2])
    load_pool = pltpu.make_async_copy(pool_ref, pool, load_sem.at[3])
    load_dkv = pltpu.make_async_copy(dkv_ref, stage_d, load_sem.at[4])
    load_queries = pltpu.make_async_copy(sq_ref, stage_q, load_sem.at[5])
    load_dq.start()
    load_queries.start()
    for c in (load_prompt, load_span, load_pool, load_dkv):
        c.start()

    load_dq.wait()
    for t in range(dq_ref.shape[0]):
        wide = stage_dq[t].astype(jnp.float32)
        for n in range(QUERY_HEADS):
            first = n // HEAD_GROUP * rows + t * HEAD_GROUP + n % HEAD_GROUP
            perm[pl.ds(first, dq_ref.shape[1], stride=rows // 2), :] = wide[
                :, n * HEAD_WIDTH : (n + 1) * HEAD_WIDTH
            ]
    dqb[0, 0] = perm[0:block, :].astype(jnp.bfloat16).reshape(dqb.shape[2:])
    load_queries.wait()
    for h in range(KEY_HEADS):
        qb[0, h // 4, pl.ds(h % 4 * rows, rows), :] = stage_q[:, pl.ds(h * HEAD_WIDTH, HEAD_WIDTH)]
    pl.semaphore_wait(barrier, 6)

    q_c, d_c, f_c, kv_c, ks_c = {}, {}, {}, {}, {}
    for o in FAR_LAST:
        q_c[o] = send(qb.at[0], qb.at[o], q_s.at[o], q_r.at[o], o, 0)
        d_c[0, o] = send(dqb.at[0, 0], dqb.at[0, o], d_s.at[0, o], d_r.at[0, o], 0, o)

    def pass_queries(oz):
        for o in near:
            d_c[o, oz] = send(dqb.at[0, oz], dqb.at[o, oz], d_s.at[o, oz], d_r.at[o, oz], o, 0)

    def pass_queries_on(oz):
        for i, o in enumerate(near):
            d_c[o, oz].wait_recv()
            f_c[oz, i] = send(
                dqb.at[o, oz, i], dqb.at[2, oz, i], f_s.at[oz, i], f_r.at[oz, i], o, 0
            )

    pass_queries(0)

    load_prompt.wait()
    start = start_ref[0]
    position = me * keys + lax.broadcasted_iota(jnp.int32, (keys, HEAD_WIDTH), 0)
    own_keys = stage[0].astype(jnp.float32)
    kv[0, 0] = jnp.where(position < start, own_keys, own_keys[0:1]).astype(jnp.bfloat16)
    kv[0, 1] = jnp.where(position < start, stage[1].astype(jnp.float32), 0.0).astype(jnp.bfloat16)
    for first in (0, 1):
        for i, o in enumerate(near):
            c = (first + i) % 2
            kv_c[o, c] = send(kv.at[0, c], kv.at[o, c], kv_s.at[o, c], kv_r.at[o, c], 0, o)
    load_span.wait()
    kvs[0] = span[...]
    for o in FAR_LAST:
        ks_c[o] = send(
            span, kvs.at[o], ks_s.at[o], ks_r.at[o], 0, o
        )

    def pass_shards_on():
        for c, o in enumerate(near):
            kv_c[o, c].wait_recv()
            kv_c[2, c] = send(kv.at[o, c], kv.at[2, c], kv_s.at[2, c], kv_r.at[2, c], 0, o)

    def load_values(oz):
        shard = y * SIDE + (z - oz + SIDE) % SIDE
        position = shard * keys + lax.broadcasted_iota(jnp.int32, (keys, HEAD_WIDTH), 0)
        vv[:, 0:HEAD_WIDTH] = kv[oz, 1]
        vv[:, HEAD_WIDTH:] = jnp.where(position < start, 1.0, 0.0).astype(jnp.bfloat16)

    def prompt_rows(oy, oz, first):
        s = dot_nt(qb[oy].reshape(block, HEAD_WIDTH), kv[oz, 0])
        top = jnp.broadcast_to(jnp.max(s, axis=1, keepdims=True), (block, HEAD_WIDTH))
        if not first:
            old = mx[oy]
            top = jnp.maximum(old, top)
        wide = jnp.concatenate([top] * (keys // HEAD_WIDTH), axis=1)
        p = jnp.exp2((s - wide) * EXP2_SCALE).astype(jnp.bfloat16)
        o = dot_nn(p, vv[...])
        if not first:
            keep = jnp.exp2((old - top) * EXP2_SCALE)
            o = o + acc[oy] * jnp.concatenate([keep, keep], axis=1)
        acc[oy] = o
        mx[oy] = top

    def prompt_block(oz):
        def step(i, _):
            prompt_rows(2 * i, oz, False)
            prompt_rows(2 * i + 1, oz, False)
            return 0

        lax.fori_loop(0, SIDE // 2, step, 0)

    def span_block(oy):
        width = SIDE * rows
        ones = jnp.ones((width, HEAD_WIDTH), jnp.bfloat16)
        values = jnp.concatenate([jnp.concatenate([kvs[o, 1] for o in range(SIDE)], axis=0), ones], axis=1)
        span_keys = jnp.concatenate([kvs[o, 0] for o in range(SIDE)], axis=0)
        row_base = ((y - oy + SIDE) % SIDE * SIDE + z) * rows

        def step(i, _):
            here = pl.ds(pl.multiple_of(i * SPAN_CHUNK, SPAN_CHUNK), SPAN_CHUNK)
            s = dot_nt(qb[oy, i], span_keys)
            row = row_base + lax.broadcasted_iota(jnp.int32, (SPAN_CHUNK, width), 0) % rows
            key = lax.broadcasted_iota(jnp.int32, (SPAN_CHUNK, width), 1)
            key = (y * SIDE + (z - key // rows + SIDE) % SIDE) * rows + key % rows
            valid = key <= row
            s = jnp.where(valid, s, MASK_NEGATIVE)
            old = mx[oy, here, :]
            top = jnp.broadcast_to(jnp.max(s, axis=1, keepdims=True), (SPAN_CHUNK, HEAD_WIDTH))
            top = jnp.maximum(old, top)
            wide = jnp.concatenate([top] * (width // HEAD_WIDTH), axis=1)
            p = jnp.where(valid, jnp.exp2((s - wide) * EXP2_SCALE), 0.0).astype(jnp.bfloat16)
            o = dot_nn(p, values)
            keep = jnp.exp2((old - top) * EXP2_SCALE)
            o = o + acc[oy, here, :] * jnp.concatenate([keep, keep], axis=1)
            total = o[:, HEAD_WIDTH:]
            pout[oy, here, :] = (o[:, :HEAD_WIDTH] / total).astype(jnp.bfloat16)
            col[here, :] = packed_stats(top, total)
            return 0

        lax.fori_loop(0, block // SPAN_CHUNK, step, 0)
        pst[oy] = jnp.transpose(col[...])[0:8]

    pair_rows = block // KEY_HEADS
    tokens = pool.shape[2]
    window = CAP * tokens

    def slots_of(home):
        def scan(b, carry):
            count, found = carry[0], carry[1:]
            hit = dest_ref[b] == home
            found = [jnp.where(hit & (count == c), b, f) for c, f in enumerate(found)]
            return (count + hit.astype(jnp.int32), *found)

        zero = jnp.int32(0)
        count, *found = lax.fori_loop(0, pool.shape[0], scan, (zero,) * (1 + CAP), unroll=4)
        fills = [jnp.where(count > c, fill_ref[f], 0) for c, f in enumerate(found)]
        return found, [request_ref[f] for f in found], fills

    def query_rows(oy, oz, h):
        half = KEY_HEADS // 2
        return dqb[oy, oz, h // half, pl.ds(h % half * pair_rows, pair_rows), :]

    def decode_home(oy, oz):
        home = (y - oy + SIDE) % SIDE * SIDE + (z - oz + SIDE) % SIDE
        index, requests, fills = slots_of(home)
        row = lax.broadcasted_iota(jnp.int32, (pair_rows, window), 0)
        key = lax.broadcasted_iota(jnp.int32, (pair_rows, window), 1)
        which = key // tokens
        request = jnp.zeros((pair_rows, window), jnp.int32)
        fill = jnp.zeros((pair_rows, window), jnp.int32)
        for c in range(CAP):
            request = jnp.where(which == c, requests[c], request)
            fill = jnp.where(which == c, fills[c], fill)
        valid = (row // (pair_rows // 2) == request) & (key % tokens < fill)
        valid_float = jnp.where(valid, 1.0, 0.0)
        ones = jnp.ones((window, HEAD_WIDTH), jnp.bfloat16)

        for h in range(KEY_HEADS):
            lanes = pl.ds(h * HEAD_WIDTH, HEAD_WIDTH)
            here = pl.ds(h * pair_rows, pair_rows)
            k = jnp.concatenate([pool[i, 0, :, lanes] for i in index], axis=0)
            v = jnp.concatenate([pool[i, 1, :, lanes] for i in index], axis=0)
            ok = valid_float > 0.5
            s = jnp.where(ok, dot_nt(query_rows(oy, oz, h), k), MASK_NEGATIVE)
            top = jnp.max(s, axis=1, keepdims=True)
            p = jnp.where(ok, jnp.exp2((s - top) * EXP2_SCALE), 0.0).astype(jnp.bfloat16)
            o = dot_nn(p, jnp.concatenate([v, ones], axis=1))
            total = o[:, HEAD_WIDTH:]
            out = o[:, :HEAD_WIDTH] / jnp.where(total > 0.0, total, 1.0)
            out = out.astype(jnp.bfloat16)
            if h < Z_ROWS // pair_rows:
                zout[oz, oy, here, :] = out
            else:
                yout[oy, oz, pl.ds(h * pair_rows - Z_ROWS, pair_rows), :] = out
            col[here, :] = packed_stats(jnp.broadcast_to(top, total.shape), total)
        stats = jnp.transpose(col[...])[0:8]
        if oy == 2:
            zfst[oz] = stats[:, :Z_ROWS]
        elif oy == 0:
            zst[oz] = stats[:, :Z_ROWS]
        for i in (0, 4):
            if oy % 2:
                zst[oz, i + oy : i + oy + 1, :] = stats[i + oy : i + oy + 1, :Z_ROWS]
            yst[oy, i + oz : i + oz + 1, :] = stats[i + oz : i + oz + 1, Z_ROWS:]

    za_c, zs_c, zf_c, ya_c, ys_c = {}, {}, {}, {}, {}
    z_part, y_part = pl.ds(0, Z_ROWS), pl.ds(Z_ROWS, block - Z_ROWS)

    def send_partials(oy, oz):
        if oz:
            za_c[oz, oy] = send(
                zout.at[oz, oy], zin.at[oz, oy], za_s.at[oz, oy], za_r.at[oz, oy],
                0, SIDE - oz,
            )
        if oy:
            ya_c[oy, oz] = send(
                yout.at[oy, oz], yin.at[oy, oz], ya_s.at[oy, oz], ya_r.at[oy, oz],
                SIDE - oy, 0,
            )

    def send_z_stats(oz):
        zs_c[oz] = send(zst.at[oz], zinst.at[oz], zs_s.at[oz], zs_r.at[oz], 0, SIDE - oz)

    def send_far_stats(oz):
        zf_c[oz] = send(zfst.at[oz], zfinst.at[oz], zf_s.at[oz], zf_r.at[oz], 0, SIDE - oz)

    def send_y_stats(oy):
        ys_c[oy] = send(yst.at[oy], yinst.at[oy], ys_s.at[oy], ys_r.at[oy], SIDE - oy, 0)

    def home(oy, oz):
        decode_home(oy, oz)
        send_partials(oy, oz)

    load_values(0)
    prompt_rows(0, 0, True)
    for oz in FAR_LAST:
        d_c[0, oz].wait_recv()
        pass_queries(oz)
    for oy in FAR_LAST:
        q_c[oy].wait_recv()
        prompt_rows(oy, 0, True)
    load_pool.wait()
    home(0, 0)
    for oz in FAR_LAST:
        home(0, oz)
    pass_queries_on(0)
    home(1, 0)
    home(3, 0)
    pass_shards_on()
    for oz in FAR_LAST:
        pass_queries_on(oz)
        home(1, oz)
        home(3, oz)
        if oz != 2:
            kv_c[oz, oz // 2 ^ 1].wait_recv()
            load_values(oz)
            prompt_block(oz)
    for o in FAR_LAST:
        send_z_stats(o)
    for oz in (1, 3, 2, 0):
        f_c[oz, 0].wait_recv()
        f_c[oz, 1].wait_recv()
        home(2, oz)
    for o in FAR_LAST:
        send_far_stats(o)
        send_y_stats(o)

    kv_c[2, 0].wait_recv()
    kv_c[2, 1].wait_recv()
    load_values(2)
    prompt_block(2)
    for oz in FAR_LAST:
        ks_c[oz].wait_recv()
    p_c = {}
    for oy in (2, 1, 3, 0):
        span_block(oy)
        if oy:
            p_c[oy, 0] = send(pout.at[oy], pin.at[oy], p_s.at[oy, 0], p_r.at[oy, 0], SIDE - oy, 0)
            p_c[oy, 1] = send(
                pst.at[oy], pinst.at[oy], p_s.at[oy, 1], p_r.at[oy, 1], SIDE - oy, 0
            )

    load_dkv.wait()
    steps, _, requests, _ = stage_d.shape
    dkv[...] = jnp.zeros_like(dkv)
    for u in range(steps):
        for c in range(2):
            new = stage_d[u, c].astype(jnp.float32)
            for h in range(KEY_HEADS):
                dkv[c, h, pl.ds(u * requests, requests), :] = new[
                    :, h * HEAD_WIDTH : (h + 1) * HEAD_WIDTH
                ]
    extra = dkv.shape[2]
    row = lax.broadcasted_iota(jnp.int32, (pair_rows, extra), 0)
    key = lax.broadcasted_iota(jnp.int32, (pair_rows, extra), 1)
    step_of_row = row % (pair_rows // 2) // HEAD_GROUP
    fresh = (row // (pair_rows // 2) == key % requests) & (key // requests <= step_of_row)
    ones = jnp.ones((extra, HEAD_WIDTH), jnp.bfloat16)
    for h in range(KEY_HEADS):
        here = pl.ds(h * pair_rows, pair_rows)
        s = jnp.where(fresh, dot_nt(query_rows(0, 0, h), dkv[0, h].astype(jnp.bfloat16)), MASK_NEGATIVE)
        top = jnp.max(s, axis=1, keepdims=True)
        p = jnp.where(fresh, jnp.exp2((s - top) * EXP2_SCALE), 0.0).astype(jnp.bfloat16)
        o = dot_nn(p, jnp.concatenate([dkv[1, h].astype(jnp.bfloat16), ones], axis=1))
        total = o[:, HEAD_WIDTH:]
        own_out[here, :] = o[:, :HEAD_WIDTH] / total
        col[here, :] = packed_stats(jnp.broadcast_to(top, total.shape), total)
    own_st[...] = jnp.transpose(col[...])[0:8]

    def spread(top, total, row):
        shape = (8, top.shape[1])
        sub = lax.broadcasted_iota(jnp.int32, shape, 0)
        return jnp.where(
            sub < 4,
            jnp.broadcast_to(top[row : row + 1], shape),
            jnp.broadcast_to(total[row : row + 1], shape),
        )

    zb_c, yb_c = {}, {}
    for oz in FAR_LAST:
        zs_c[oz].wait_recv()
    shares, top, total = join([zst[0]] + [zinst[oz] for oz in FAR_LAST])
    for oy in (1, 3, 0, 2):
        if oy == 2:
            for oz in FAR_LAST:
                zf_c[oz].wait_recv()
            shares, top, total = join([zfst[0]] + [zfinst[oz] for oz in FAR_LAST])
        for oz in FAR_LAST:
            za_c[oz, oy].wait_recv()
        out = blend(
            shares, oy,
            [lambda oy=oy: zout[0, oy]]
            + [lambda oz=oz, oy=oy: zin[oz, oy] for oz in FAR_LAST],
        )
        zb[oy] = out.astype(jnp.bfloat16)
        zbst[oy] = spread(top, total, oy)
        if oy:
            zb_c[oy, 0] = send(zb.at[oy], zbin.at[oy], zb_s.at[oy, 0], zb_r.at[oy, 0], SIDE - oy, 0)
            zb_c[oy, 1] = send(
                zbst.at[oy], zbinst.at[oy], zb_s.at[oy, 1], zb_r.at[oy, 1], SIDE - oy, 0
            )
    for oy in FAR_LAST:
        ys_c[oy].wait_recv()
    shares, top, total = join([yst[0]] + [yinst[oy] for oy in FAR_LAST])
    for oz in (1, 3, 2, 0):
        for oy in FAR_LAST:
            ya_c[oy, oz].wait_recv()
        out = blend(
            shares, oz,
            [lambda oz=oz: yout[0, oz]]
            + [lambda oz=oz, oy=oy: yin[oy, oz] for oy in FAR_LAST],
        )
        yb[oz] = out.astype(jnp.bfloat16)
        ybst[oz] = spread(top, total, oz)
        if oz:
            yb_c[oz, 0] = send(yb.at[oz], ybin.at[oz], yb_s.at[oz, 0], yb_r.at[oz, 0], 0, SIDE - oz)
            yb_c[oz, 1] = send(
                ybst.at[oz], ybinst.at[oz], yb_s.at[oz, 1], yb_r.at[oz, 1], 0, SIDE - oz
            )

    for oy in FAR_LAST:
        p_c[oy, 0].wait_recv()
        p_c[oy, 1].wait_recv()
    shares, _, _ = join([pst[0]] + [pinst[oy] for oy in FAR_LAST])
    out = blend(shares, 0, [lambda: pout[0]] + [lambda oy=oy: pin[oy] for oy in FAR_LAST])
    out = out.astype(jnp.bfloat16)
    for h in range(KEY_HEADS):
        att_ref[:, pl.ds(h * HEAD_WIDTH, HEAD_WIDTH)] = out[h * rows : (h + 1) * rows]

    for c in list(zb_c.values()) + list(yb_c.values()):
        c.wait_recv()
    for part, n, part_out, part_st, into, into_st in (
        (z_part, Z_ROWS, zb, zbst, zbin, zbinst),
        (y_part, block - Z_ROWS, yb, ybst, ybin, ybinst),
    ):
        shares, _, _ = join(
            [own_st[:, part], part_st[0]] + [into_st[o] for o in FAR_LAST]
        )
        out = blend(
            shares, 0,
            [lambda part=part: own_out[part, :], lambda part_out=part_out: part_out[0]]
            + [lambda o=o, into=into: into[o] for o in FAR_LAST],
        )
        perm[part, :] = out

    half_pair = pair_rows // 2
    for t in range(steps):
        for h in range(KEY_HEADS):
            pieces = [
                perm[pl.ds(h * pair_rows + t * HEAD_GROUP + g, requests, stride=half_pair), :]
                for g in range(HEAD_GROUP)
            ]
            lanes = pl.ds(h * HEAD_GROUP * HEAD_WIDTH, HEAD_GROUP * HEAD_WIDTH)
            dec_ref[t, :, lanes] = jnp.concatenate(pieces, axis=1).astype(jnp.bfloat16)

    for c in sent:
        c.wait_send()


def on_device(
    span_queries,
    span_key_value,
    prompt_key_value,
    span_start,
    block_pool_key_value,
    block_dest,
    block_request,
    block_fill,
    decode_query,
    decoded_key_value,
):
    steps, requests = decode_query.shape[:2]
    rows = span_queries.shape[0]
    block = KEY_HEADS * rows
    keys = prompt_key_value.shape[1]
    halves = (2, block // 2, HEAD_WIDTH)
    decoded = decoded_key_value.shape

    bf, f32 = jnp.bfloat16, jnp.float32
    part = (block, HEAD_WIDTH)
    z_part, y_part = (Z_ROWS, HEAD_WIDTH), (block - Z_ROWS, HEAD_WIDTH)
    stat, z_stat, y_stat = (8, block), (8, Z_ROWS), (8, block - Z_ROWS)
    vmem = pl.BlockSpec(memory_space=pltpu.VMEM)
    smem = pl.BlockSpec(memory_space=pltpu.SMEM)
    hbm = pl.BlockSpec(memory_space=pltpu.HBM)
    dma = pltpu.SemaphoreType.DMA
    one, two = (SIDE,), (SIDE, SIDE)
    buffers = [
        ((2, keys, HEAD_WIDTH), bf),
        (span_queries.shape, bf),
        ((2, rows, HEAD_WIDTH), bf),
        (one + halves, bf),
        ((SIDE, 2, keys, HEAD_WIDTH), bf),
        ((SIDE, 2, rows, HEAD_WIDTH), bf),
        ((keys, 2 * HEAD_WIDTH), bf),
        (two + halves, bf),
        (decoded, bf), (decode_query.shape, bf),
        ((2, KEY_HEADS, 2 * steps * requests, HEAD_WIDTH), f32),
        (block_pool_key_value.shape, bf),
        ((SIDE, block, 2 * HEAD_WIDTH), f32),
        (one + part, f32),
        (part, f32),
        (one + part, bf), (one + stat, f32),
        (one + part, bf), (one + stat, f32),
        (two + z_part, bf), (two + y_part, bf),
        (one + z_stat, f32), (one + z_stat, f32), (one + y_stat, f32),
        (two + z_part, bf), (one + z_stat, f32), (one + z_stat, f32),
        (two + y_part, bf), (one + y_stat, f32),
        (one + z_part, bf), (one + z_stat, f32),
        (one + z_part, bf), (one + z_stat, f32),
        (one + y_part, bf), (one + y_stat, f32),
        (one + y_part, bf), (one + y_stat, f32),
        (part, f32), (stat, f32),
        ((block + rows, HEAD_WIDTH), f32),
    ]
    pairs = [one, (SIDE, 2), one, two, (SIDE, 2), (SIDE, 2), two, one, one, two, one, (SIDE, 2), (SIDE, 2)]
    semaphores = [dma((6,))]
    for shape in pairs:
        semaphores += [dma(shape), dma(shape)]
    attended, dec = pl.pallas_call(
        fused_kernel,
        out_shape=(
            jax.ShapeDtypeStruct(span_queries.shape, bf),
            jax.ShapeDtypeStruct(decode_query.shape, bf),
        ),
        in_specs=[hbm, hbm, hbm, smem, hbm, smem, smem, smem, hbm, hbm],
        out_specs=(vmem, vmem),
        scratch_shapes=[pltpu.VMEM(shape, dtype) for shape, dtype in buffers] + semaphores,
        compiler_params=pltpu.CompilerParams(
            collective_id=0, has_side_effects=True, vmem_limit_bytes=64 * 1024 * 1024 - 65536
        ),
        name="span_and_decode",
    )(span_queries, span_key_value, prompt_key_value, span_start, block_pool_key_value, block_dest[:, 0],
      block_request, block_fill, decode_query, decoded_key_value)
    return attended, dec


def solution(mesh):
    placed = (
        P("seq", "req"),
        P(None, "seq", "req"),
        P(None, "seq", "req"),
        P(),
        P(("seq", "req"), None, None, None),
        P(("seq", "req"), None),
        P(("seq", "req")),
        P(("seq", "req")),
        P(None, ("seq", "req"), None),
        P(None, None, ("seq", "req"), None),
    )
    return jax.shard_map(
        on_device,
        mesh=mesh,
        in_specs=placed,
        out_specs=(P("seq", "req"), P(None, ("seq", "req"), None)),
        check_vma=False,
    )
```

```python
import functools

import jax
import jax.numpy as jnp
from jax import lax
from jax.experimental import pallas as pl
from jax.experimental.pallas import tpu as pltpu
from jax.sharding import PartitionSpec as P

QUERY_HEADS = 64
KEY_HEADS = 8
HEAD_WIDTH = 128
HEAD_GROUP = QUERY_HEADS // KEY_HEADS
CAP = 4
SIDE = 4
HOMES = SIDE * SIDE

MASK_NEGATIVE = -1e30
EXP2_SCALE = HEAD_WIDTH ** (-0.5) * 1.4426950408889634
FAR_LAST = (1, 3, 2)
SPAN_CHUNK = 256
Z_ROWS = 256


def dot_nt(a, b):
    return lax.dot_general(a, b, (((1,), (1,)), ((), ())), preferred_element_type=jnp.float32)


def dot_nn(a, b):
    return lax.dot_general(a, b, (((1,), (0,)), ((), ())), preferred_element_type=jnp.float32)


def packed_stats(top, total):
    lane = lax.broadcasted_iota(jnp.int32, top.shape, 1)
    return jnp.where(lane < 4, top, total)


def join(stats):
    tops = [s[0:4] for s in stats]
    top = functools.reduce(jnp.maximum, tops)
    weights = [jnp.exp2((t - top) * EXP2_SCALE) * s[4:8] for t, s in zip(tops, stats)]
    total = functools.reduce(jnp.add, weights)
    inverse = 1.0 / jnp.where(total > 0.0, total, 1.0)
    return [w * inverse for w in weights], top, total


def blend(shares, row, parts):
    out = None
    for share, part in zip(shares, parts):
        wide = jnp.broadcast_to(share[row : row + 1], (HEAD_WIDTH, share.shape[1]))
        term = jnp.transpose(wide) * part().astype(jnp.float32)
        out = term if out is None else out + term
    return out


def fused_kernel(
    sq_ref, skv_ref, pkv_ref, start_ref, pool_ref, dest_ref, request_ref, fill_ref, dq_ref, dkv_ref,
    att_ref, dec_ref,
    stage, stage_q, span, qb, kv, kvs, vv, dqb, stage_d, stage_dq, dkv, pool, acc, mx, col,
    pout, pst, pin, pinst,
    zout, yout, zst, zfst, yst, zin, zinst, zfinst, yin, yinst,
    zb, zbst, zbin, zbinst, yb, ybst, ybin, ybinst,
    own_out, own_st, perm,
    load_sem, q_s, q_r, kv_s, kv_r, ks_s, ks_r, d_s, d_r, f_s, f_r, p_s, p_r,
    za_s, za_r, zs_s, zs_r, zf_s, zf_r, ya_s, ya_r, ys_s, ys_r, zb_s, zb_r, yb_s, yb_r,
):
    me = lax.axis_index("seq")
    y, z = me // SIDE, me % SIDE
    rows = sq_ref.shape[0]
    block = KEY_HEADS * rows
    keys = pkv_ref.shape[1]
    mesh_id = pl.DeviceIdType.MESH
    near = (1, 3)

    def at(dy, dz):
        return {"seq": (y + dy) % SIDE * SIDE + (z + dz) % SIDE}

    def remote(src, dst, send, recv, dy, dz):
        return pltpu.make_async_remote_copy(
            src_ref=src, dst_ref=dst, send_sem=send, recv_sem=recv,
            device_id=at(dy, dz), device_id_type=mesh_id,
        )

    sent = []

    def send(*args):
        copy = remote(*args)
        copy.start()
        sent.append(copy)
        return copy

    barrier = pltpu.get_barrier_semaphore()
    for o in (1, 2, 3):
        pl.semaphore_signal(barrier, inc=1, device_id=at(o, 0), device_id_type=mesh_id)
        pl.semaphore_signal(barrier, inc=1, device_id=at(0, o), device_id_type=mesh_id)

    load_prompt = pltpu.make_async_copy(pkv_ref, stage, load_sem.at[0])
    load_dq = pltpu.make_async_copy(dq_ref, stage_dq, load_sem.at[1])
    load_span = pltpu.make_async_copy(skv_ref, span, load_sem.at[2])
    load_pool = pltpu.make_async_copy(pool_ref, pool, load_sem.at[3])
    load_dkv = pltpu.make_async_copy(dkv_ref, stage_d, load_sem.at[4])
    load_queries = pltpu.make_async_copy(sq_ref, stage_q, load_sem.at[5])
    load_dq.start()
    load_queries.start()
    for c in (load_prompt, load_span, load_pool, load_dkv):
        c.start()

    load_dq.wait()
    for t in range(dq_ref.shape[0]):
        wide = stage_dq[t].astype(jnp.float32)
        for n in range(QUERY_HEADS):
            first = n // HEAD_GROUP * rows + t * HEAD_GROUP + n % HEAD_GROUP
            perm[pl.ds(first, dq_ref.shape[1], stride=rows // 2), :] = wide[
                :, n * HEAD_WIDTH : (n + 1) * HEAD_WIDTH
            ]
    dqb[0, 0] = perm[0:block, :].astype(jnp.bfloat16).reshape(dqb.shape[2:])
    load_queries.wait()
    for h in range(KEY_HEADS):
        qb[0, h // 4, pl.ds(h % 4 * rows, rows), :] = stage_q[:, pl.ds(h * HEAD_WIDTH, HEAD_WIDTH)]
    load_prompt.wait()
    start = start_ref[0]
    position = me * keys + lax.broadcasted_iota(jnp.int32, (keys, HEAD_WIDTH), 0)
    own_keys = stage[0].astype(jnp.float32)
    kv[0, 0] = jnp.where(position < start, own_keys, own_keys[0:1]).astype(jnp.bfloat16)
    kv[0, 1] = jnp.where(position < start, stage[1].astype(jnp.float32), 0.0).astype(jnp.bfloat16)
    load_span.wait()
    kvs[0] = span[...]
    pl.semaphore_wait(barrier, 6)

    q_c, d_c, f_c, kv_c, ks_c = {}, {}, {}, {}, {}
    for o in FAR_LAST:
        d_c[0, o] = send(dqb.at[0, 0], dqb.at[0, o], d_s.at[0, o], d_r.at[0, o], 0, o)
    for first in (0, 1):
        for i, o in enumerate(near):
            c = (first + i) % 2
            kv_c[o, c] = send(kv.at[0, c], kv.at[o, c], kv_s.at[o, c], kv_r.at[o, c], 0, o)
    for o in FAR_LAST:
        q_c[o] = send(qb.at[0], qb.at[o], q_s.at[o], q_r.at[o], o, 0)

    def pass_queries(oz):
        for o in near:
            d_c[o, oz] = send(dqb.at[0, oz], dqb.at[o, oz], d_s.at[o, oz], d_r.at[o, oz], o, 0)

    def pass_queries_on(oz):
        for i, o in enumerate(near):
            d_c[o, oz].wait_recv()
            f_c[oz, i] = send(
                dqb.at[o, oz, i], dqb.at[2, oz, i], f_s.at[oz, i], f_r.at[oz, i], o, 0
            )

    pass_queries(0)

    for o in FAR_LAST:
        ks_c[o] = send(
            span, kvs.at[o], ks_s.at[o], ks_r.at[o], 0, o
        )

    def pass_shards_on():
        for c, o in enumerate(near):
            kv_c[o, c].wait_recv()
            kv_c[2, c] = send(kv.at[o, c], kv.at[2, c], kv_s.at[2, c], kv_r.at[2, c], 0, o)

    def load_values(oz):
        shard = y * SIDE + (z - oz + SIDE) % SIDE
        position = shard * keys + lax.broadcasted_iota(jnp.int32, (keys, HEAD_WIDTH), 0)
        vv[:, 0:HEAD_WIDTH] = kv[oz, 1]
        vv[:, HEAD_WIDTH:] = jnp.where(position < start, 1.0, 0.0).astype(jnp.bfloat16)

    def prompt_rows(oy, oz, first):
        s = dot_nt(qb[oy].reshape(block, HEAD_WIDTH), kv[oz, 0])
        top = jnp.broadcast_to(jnp.max(s, axis=1, keepdims=True), (block, HEAD_WIDTH))
        if not first:
            old = mx[oy]
            top = jnp.maximum(old, top)
        wide = jnp.concatenate([top] * (keys // HEAD_WIDTH), axis=1)
        p = jnp.exp2((s - wide) * EXP2_SCALE).astype(jnp.bfloat16)
        o = dot_nn(p, vv[...])
        if not first:
            keep = jnp.exp2((old - top) * EXP2_SCALE)
            o = o + acc[oy] * jnp.concatenate([keep, keep], axis=1)
        acc[oy] = o
        mx[oy] = top

    def prompt_block(oz):
        def step(i, _):
            prompt_rows(2 * i, oz, False)
            prompt_rows(2 * i + 1, oz, False)
            return 0

        lax.fori_loop(0, SIDE // 2, step, 0)

    def span_block(oy):
        width = SIDE * rows
        ones = jnp.ones((width, HEAD_WIDTH), jnp.bfloat16)
        values = jnp.concatenate([jnp.concatenate([kvs[o, 1] for o in range(SIDE)], axis=0), ones], axis=1)
        span_keys = jnp.concatenate([kvs[o, 0] for o in range(SIDE)], axis=0)
        row_base = ((y - oy + SIDE) % SIDE * SIDE + z) * rows

        def step(i, _):
            here = pl.ds(pl.multiple_of(i * SPAN_CHUNK, SPAN_CHUNK), SPAN_CHUNK)
            s = dot_nt(qb[oy, i], span_keys)
            row = row_base + lax.broadcasted_iota(jnp.int32, (SPAN_CHUNK, width), 0) % rows
            key = lax.broadcasted_iota(jnp.int32, (SPAN_CHUNK, width), 1)
            key = (y * SIDE + (z - key // rows + SIDE) % SIDE) * rows + key % rows
            valid = key <= row
            s = jnp.where(valid, s, MASK_NEGATIVE)
            old = mx[oy, here, :]
            top = jnp.broadcast_to(jnp.max(s, axis=1, keepdims=True), (SPAN_CHUNK, HEAD_WIDTH))
            top = jnp.maximum(old, top)
            wide = jnp.concatenate([top] * (width // HEAD_WIDTH), axis=1)
            p = jnp.where(valid, jnp.exp2((s - wide) * EXP2_SCALE), 0.0).astype(jnp.bfloat16)
            o = dot_nn(p, values)
            keep = jnp.exp2((old - top) * EXP2_SCALE)
            o = o + acc[oy, here, :] * jnp.concatenate([keep, keep], axis=1)
            total = o[:, HEAD_WIDTH:]
            pout[oy, here, :] = (o[:, :HEAD_WIDTH] / total).astype(jnp.bfloat16)
            col[here, :] = packed_stats(top, total)
            return 0

        lax.fori_loop(0, block // SPAN_CHUNK, step, 0)
        pst[oy] = jnp.transpose(col[...])[0:8]

    pair_rows = block // KEY_HEADS
    tokens = pool.shape[2]
    window = CAP * tokens

    def slots_of(home):
        def scan(b, carry):
            count, found = carry[0], carry[1:]
            hit = dest_ref[b] == home
            found = [jnp.where(hit & (count == c), b, f) for c, f in enumerate(found)]
            return (count + hit.astype(jnp.int32), *found)

        zero = jnp.int32(0)
        count, *found = lax.fori_loop(0, pool.shape[0], scan, (zero,) * (1 + CAP), unroll=4)
        fills = [jnp.where(count > c, fill_ref[f], 0) for c, f in enumerate(found)]
        return found, [request_ref[f] for f in found], fills

    def query_rows(oy, oz, h):
        half = KEY_HEADS // 2
        return dqb[oy, oz, h // half, pl.ds(h % half * pair_rows, pair_rows), :]

    def decode_home(oy, oz):
        home = (y - oy + SIDE) % SIDE * SIDE + (z - oz + SIDE) % SIDE
        index, requests, fills = slots_of(home)
        row = lax.broadcasted_iota(jnp.int32, (pair_rows, window), 0)
        key = lax.broadcasted_iota(jnp.int32, (pair_rows, window), 1)
        which = key // tokens
        request = jnp.zeros((pair_rows, window), jnp.int32)
        fill = jnp.zeros((pair_rows, window), jnp.int32)
        for c in range(CAP):
            request = jnp.where(which == c, requests[c], request)
            fill = jnp.where(which == c, fills[c], fill)
        valid = (row // (pair_rows // 2) == request) & (key % tokens < fill)
        valid_float = jnp.where(valid, 1.0, 0.0)
        ones = jnp.ones((window, HEAD_WIDTH), jnp.bfloat16)

        for h in range(KEY_HEADS):
            lanes = pl.ds(h * HEAD_WIDTH, HEAD_WIDTH)
            here = pl.ds(h * pair_rows, pair_rows)
            k = jnp.concatenate([pool[i, 0, :, lanes] for i in index], axis=0)
            v = jnp.concatenate([pool[i, 1, :, lanes] for i in index], axis=0)
            ok = valid_float > 0.5
            s = jnp.where(ok, dot_nt(query_rows(oy, oz, h), k), MASK_NEGATIVE)
            top = jnp.max(s, axis=1, keepdims=True)
            p = jnp.where(ok, jnp.exp2((s - top) * EXP2_SCALE), 0.0).astype(jnp.bfloat16)
            o = dot_nn(p, jnp.concatenate([v, ones], axis=1))
            total = o[:, HEAD_WIDTH:]
            out = o[:, :HEAD_WIDTH] / jnp.where(total > 0.0, total, 1.0)
            out = out.astype(jnp.bfloat16)
            if h < Z_ROWS // pair_rows:
                zout[oz, oy, here, :] = out
            else:
                yout[oy, oz, pl.ds(h * pair_rows - Z_ROWS, pair_rows), :] = out
            col[here, :] = packed_stats(jnp.broadcast_to(top, total.shape), total)
        stats = jnp.transpose(col[...])[0:8]
        if oy == 2:
            zfst[oz] = stats[:, :Z_ROWS]
        elif oy == 0:
            zst[oz] = stats[:, :Z_ROWS]
        for i in (0, 4):
            if oy % 2:
                zst[oz, i + oy : i + oy + 1, :] = stats[i + oy : i + oy + 1, :Z_ROWS]
            yst[oy, i + oz : i + oz + 1, :] = stats[i + oz : i + oz + 1, Z_ROWS:]

    za_c, zs_c, zf_c, ya_c, ys_c = {}, {}, {}, {}, {}
    z_part, y_part = pl.ds(0, Z_ROWS), pl.ds(Z_ROWS, block - Z_ROWS)

    def send_partials(oy, oz):
        if oz:
            za_c[oz, oy] = send(
                zout.at[oz, oy], zin.at[oz, oy], za_s.at[oz, oy], za_r.at[oz, oy],
                0, SIDE - oz,
            )
        if oy:
            ya_c[oy, oz] = send(
                yout.at[oy, oz], yin.at[oy, oz], ya_s.at[oy, oz], ya_r.at[oy, oz],
                SIDE - oy, 0,
            )

    def send_z_stats(oz):
        zs_c[oz] = send(zst.at[oz], zinst.at[oz], zs_s.at[oz], zs_r.at[oz], 0, SIDE - oz)

    def send_far_stats(oz):
        zf_c[oz] = send(zfst.at[oz], zfinst.at[oz], zf_s.at[oz], zf_r.at[oz], 0, SIDE - oz)

    def send_y_stats(oy):
        ys_c[oy] = send(yst.at[oy], yinst.at[oy], ys_s.at[oy], ys_r.at[oy], SIDE - oy, 0)

    def home(oy, oz):
        decode_home(oy, oz)
        send_partials(oy, oz)

    load_values(0)
    prompt_rows(0, 0, True)
    for oz in FAR_LAST:
        d_c[0, oz].wait_recv()
        pass_queries(oz)
    for oy in FAR_LAST:
        q_c[oy].wait_recv()
        prompt_rows(oy, 0, True)
    load_pool.wait()
    home(0, 0)
    for oz in FAR_LAST:
        decode_home(0, oz)
    pass_queries_on(0)
    home(1, 0)
    home(3, 0)
    pass_shards_on()
    for oz in FAR_LAST:
        send_partials(0, oz)
    for oz in FAR_LAST:
        pass_queries_on(oz)
        home(1, oz)
        home(3, oz)
        if oz != 2:
            kv_c[oz, oz // 2 ^ 1].wait_recv()
            load_values(oz)
            prompt_block(oz)
    for o in FAR_LAST:
        send_z_stats(o)
    for oz in (1, 3, 2, 0):
        f_c[oz, 0].wait_recv()
        f_c[oz, 1].wait_recv()
        home(2, oz)
    for o in FAR_LAST:
        send_far_stats(o)
        send_y_stats(o)

    kv_c[2, 0].wait_recv()
    kv_c[2, 1].wait_recv()
    load_values(2)
    prompt_block(2)
    for oz in FAR_LAST:
        ks_c[oz].wait_recv()
    p_c = {}
    for oy in (2, 1, 3, 0):
        span_block(oy)
        if oy:
            p_c[oy, 0] = send(pout.at[oy], pin.at[oy], p_s.at[oy, 0], p_r.at[oy, 0], SIDE - oy, 0)
            p_c[oy, 1] = send(
                pst.at[oy], pinst.at[oy], p_s.at[oy, 1], p_r.at[oy, 1], SIDE - oy, 0
            )

    load_dkv.wait()
    steps, _, requests, _ = stage_d.shape
    dkv[...] = jnp.zeros_like(dkv)
    for u in range(steps):
        for c in range(2):
            new = stage_d[u, c].astype(jnp.float32)
            for h in range(KEY_HEADS):
                dkv[c, h, pl.ds(u * requests, requests), :] = new[
                    :, h * HEAD_WIDTH : (h + 1) * HEAD_WIDTH
                ]
    extra = dkv.shape[2]
    row = lax.broadcasted_iota(jnp.int32, (pair_rows, extra), 0)
    key = lax.broadcasted_iota(jnp.int32, (pair_rows, extra), 1)
    step_of_row = row % (pair_rows // 2) // HEAD_GROUP
    fresh = (row // (pair_rows // 2) == key % requests) & (key // requests <= step_of_row)
    ones = jnp.ones((extra, HEAD_WIDTH), jnp.bfloat16)
    for h in range(KEY_HEADS):
        here = pl.ds(h * pair_rows, pair_rows)
        s = jnp.where(fresh, dot_nt(query_rows(0, 0, h), dkv[0, h].astype(jnp.bfloat16)), MASK_NEGATIVE)
        top = jnp.max(s, axis=1, keepdims=True)
        p = jnp.where(fresh, jnp.exp2((s - top) * EXP2_SCALE), 0.0).astype(jnp.bfloat16)
        o = dot_nn(p, jnp.concatenate([dkv[1, h].astype(jnp.bfloat16), ones], axis=1))
        total = o[:, HEAD_WIDTH:]
        own_out[here, :] = o[:, :HEAD_WIDTH] / total
        col[here, :] = packed_stats(jnp.broadcast_to(top, total.shape), total)
    own_st[...] = jnp.transpose(col[...])[0:8]

    def spread(top, total, row):
        shape = (8, top.shape[1])
        sub = lax.broadcasted_iota(jnp.int32, shape, 0)
        return jnp.where(
            sub < 4,
            jnp.broadcast_to(top[row : row + 1], shape),
            jnp.broadcast_to(total[row : row + 1], shape),
        )

    zb_c, yb_c = {}, {}
    for oz in FAR_LAST:
        zs_c[oz].wait_recv()
    shares, top, total = join([zst[0]] + [zinst[oz] for oz in FAR_LAST])
    for oy in (1, 3, 0, 2):
        if oy == 2:
            for oz in FAR_LAST:
                zf_c[oz].wait_recv()
            shares, top, total = join([zfst[0]] + [zfinst[oz] for oz in FAR_LAST])
        for oz in FAR_LAST:
            za_c[oz, oy].wait_recv()
        out = blend(
            shares, oy,
            [lambda oy=oy: zout[0, oy]]
            + [lambda oz=oz, oy=oy: zin[oz, oy] for oz in FAR_LAST],
        )
        zb[oy] = out.astype(jnp.bfloat16)
        zbst[oy] = spread(top, total, oy)
        if oy:
            zb_c[oy, 0] = send(zb.at[oy], zbin.at[oy], zb_s.at[oy, 0], zb_r.at[oy, 0], SIDE - oy, 0)
            zb_c[oy, 1] = send(
                zbst.at[oy], zbinst.at[oy], zb_s.at[oy, 1], zb_r.at[oy, 1], SIDE - oy, 0
            )
    for oy in FAR_LAST:
        ys_c[oy].wait_recv()
    shares, top, total = join([yst[0]] + [yinst[oy] for oy in FAR_LAST])
    for oz in (1, 3, 2, 0):
        for oy in FAR_LAST:
            ya_c[oy, oz].wait_recv()
        out = blend(
            shares, oz,
            [lambda oz=oz: yout[0, oz]]
            + [lambda oz=oz, oy=oy: yin[oy, oz] for oy in FAR_LAST],
        )
        yb[oz] = out.astype(jnp.bfloat16)
        ybst[oz] = spread(top, total, oz)
        if oz:
            yb_c[oz, 0] = send(yb.at[oz], ybin.at[oz], yb_s.at[oz, 0], yb_r.at[oz, 0], 0, SIDE - oz)
            yb_c[oz, 1] = send(
                ybst.at[oz], ybinst.at[oz], yb_s.at[oz, 1], yb_r.at[oz, 1], 0, SIDE - oz
            )

    for oy in FAR_LAST:
        p_c[oy, 0].wait_recv()
        p_c[oy, 1].wait_recv()
    shares, _, _ = join([pst[0]] + [pinst[oy] for oy in FAR_LAST])
    out = blend(shares, 0, [lambda: pout[0]] + [lambda oy=oy: pin[oy] for oy in FAR_LAST])
    out = out.astype(jnp.bfloat16)
    for h in range(KEY_HEADS):
        att_ref[:, pl.ds(h * HEAD_WIDTH, HEAD_WIDTH)] = out[h * rows : (h + 1) * rows]

    for c in list(zb_c.values()) + list(yb_c.values()):
        c.wait_recv()
    for part, n, part_out, part_st, into, into_st in (
        (z_part, Z_ROWS, zb, zbst, zbin, zbinst),
        (y_part, block - Z_ROWS, yb, ybst, ybin, ybinst),
    ):
        shares, _, _ = join(
            [own_st[:, part], part_st[0]] + [into_st[o] for o in FAR_LAST]
        )
        out = blend(
            shares, 0,
            [lambda part=part: own_out[part, :], lambda part_out=part_out: part_out[0]]
            + [lambda o=o, into=into: into[o] for o in FAR_LAST],
        )
        perm[part, :] = out

    half_pair = pair_rows // 2
    for t in range(steps):
        for h in range(KEY_HEADS):
            pieces = [
                perm[pl.ds(h * pair_rows + t * HEAD_GROUP + g, requests, stride=half_pair), :]
                for g in range(HEAD_GROUP)
            ]
            lanes = pl.ds(h * HEAD_GROUP * HEAD_WIDTH, HEAD_GROUP * HEAD_WIDTH)
            dec_ref[t, :, lanes] = jnp.concatenate(pieces, axis=1).astype(jnp.bfloat16)

    for c in sent:
        c.wait_send()


def on_device(
    span_queries,
    span_key_value,
    prompt_key_value,
    span_start,
    block_pool_key_value,
    block_dest,
    block_request,
    block_fill,
    decode_query,
    decoded_key_value,
):
    steps, requests = decode_query.shape[:2]
    rows = span_queries.shape[0]
    block = KEY_HEADS * rows
    keys = prompt_key_value.shape[1]
    halves = (2, block // 2, HEAD_WIDTH)
    decoded = decoded_key_value.shape

    bf, f32 = jnp.bfloat16, jnp.float32
    part = (block, HEAD_WIDTH)
    z_part, y_part = (Z_ROWS, HEAD_WIDTH), (block - Z_ROWS, HEAD_WIDTH)
    stat, z_stat, y_stat = (8, block), (8, Z_ROWS), (8, block - Z_ROWS)
    vmem = pl.BlockSpec(memory_space=pltpu.VMEM)
    smem = pl.BlockSpec(memory_space=pltpu.SMEM)
    hbm = pl.BlockSpec(memory_space=pltpu.HBM)
    dma = pltpu.SemaphoreType.DMA
    one, two = (SIDE,), (SIDE, SIDE)
    buffers = [
        ((2, keys, HEAD_WIDTH), bf),
        (span_queries.shape, bf),
        ((2, rows, HEAD_WIDTH), bf),
        (one + halves, bf),
        ((SIDE, 2, keys, HEAD_WIDTH), bf),
        ((SIDE, 2, rows, HEAD_WIDTH), bf),
        ((keys, 2 * HEAD_WIDTH), bf),
        (two + halves, bf),
        (decoded, bf), (decode_query.shape, bf),
        ((2, KEY_HEADS, 2 * steps * requests, HEAD_WIDTH), f32),
        (block_pool_key_value.shape, bf),
        ((SIDE, block, 2 * HEAD_WIDTH), f32),
        (one + part, f32),
        (part, f32),
        (one + part, bf), (one + stat, f32),
        (one + part, bf), (one + stat, f32),
        (two + z_part, bf), (two + y_part, bf),
        (one + z_stat, f32), (one + z_stat, f32), (one + y_stat, f32),
        (two + z_part, bf), (one + z_stat, f32), (one + z_stat, f32),
        (two + y_part, bf), (one + y_stat, f32),
        (one + z_part, bf), (one + z_stat, f32),
        (one + z_part, bf), (one + z_stat, f32),
        (one + y_part, bf), (one + y_stat, f32),
        (one + y_part, bf), (one + y_stat, f32),
        (part, f32), (stat, f32),
        ((block + rows, HEAD_WIDTH), f32),
    ]
    pairs = [one, (SIDE, 2), one, two, (SIDE, 2), (SIDE, 2), two, one, one, two, one, (SIDE, 2), (SIDE, 2)]
    semaphores = [dma((6,))]
    for shape in pairs:
        semaphores += [dma(shape), dma(shape)]
    attended, dec = pl.pallas_call(
        fused_kernel,
        out_shape=(
            jax.ShapeDtypeStruct(span_queries.shape, bf),
            jax.ShapeDtypeStruct(decode_query.shape, bf),
        ),
        in_specs=[hbm, hbm, hbm, smem, hbm, smem, smem, smem, hbm, hbm],
        out_specs=(vmem, vmem),
        scratch_shapes=[pltpu.VMEM(shape, dtype) for shape, dtype in buffers] + semaphores,
        compiler_params=pltpu.CompilerParams(
            collective_id=0, has_side_effects=True, vmem_limit_bytes=64 * 1024 * 1024 - 65536
        ),
        name="span_and_decode",
    )(span_queries, span_key_value, prompt_key_value, span_start, block_pool_key_value, block_dest[:, 0],
      block_request, block_fill, decode_query, decoded_key_value)
    return attended, dec


def solution(mesh):
    placed = (
        P("seq", "req"),
        P(None, "seq", "req"),
        P(None, "seq", "req"),
        P(),
        P(("seq", "req"), None, None, None),
        P(("seq", "req"), None),
        P(("seq", "req")),
        P(("seq", "req")),
        P(None, ("seq", "req"), None),
        P(None, None, ("seq", "req"), None),
    )
    return jax.shard_map(
        on_device,
        mesh=mesh,
        in_specs=placed,
        out_specs=(P("seq", "req"), P(None, ("seq", "req"), None)),
        check_vma=False,
    )
```
